32 devices in a mesh: pair: 8 (over y, x, core), win: 4 (over z).
Axes of the slice: x: 2, y: 2, z: 4, core: 2. Of those that a mesh axis runs over, the one named last changes fastest.
Arguments:
- traces: bfloat16 [2048, 128, 1024], P('pair', 'win'), may hold values from -210 to 210, as said below
- partner: int32 [2, 8], replicated, may hold values from 0 to 7, as said below
- block_ids: int32 [8], replicated, may hold values from 0 to 7, each once
Outputs:
- correlations: float32 [2, 32, 2, 2048, 256], P(None, 'win', None, 'pair')
The draws below stay inside these ranges and needn't reach their ends.
Inputs may be any that keep to these rules, and one draw needn't show every extreme that they name: traces are noise whose amplitude and spectral colour vary from channel to channel and window to window. Each row of partner pairs every fibre block with one other block: partner[r, partner[r, b]] = b and partner[r, b] != b; the rows are distinct rounds of one round-robin plan. block_ids names each fibre block once.
All inputs are finite; a program needn't handle non-finite values.
Results may differ from the reference program's by a relative error of at most 0.0058.
Values may be sent and summed in bfloat16 or wider, within the bound.
No kernel may reach another device: no remote copies, remote signals or barrier semaphores. Data moves between devices by JAX's collectives and lax.ppermute only.
A program may use at most 128 MiB of HBM per device.

```python
import math
import jax
import jax.numpy as jnp
from jax import lax

BLK = 256
SAMPLES = 1024
BINS = 32
FIRST_BIN = 16
BIN_STEP = 8
ROUNDS = 2
CHANNELS = 2048
WINDOWS = 128
N_PAIR = 8


def draw_traces(key, part):
    keys = jax.random.split(key, 5)
    full_shape = (CHANNELS, WINDOWS, SAMPLES + 2)
    base = jnp.clip(jax.random.normal(keys[0], full_shape, jnp.float32), -5.0, 5.0)
    spread = math.log(10.0)
    first_tap = jax.random.uniform(keys[2], (CHANNELS, WINDOWS, 1), jnp.float32, -0.9, 0.9)
    second_tap = jax.random.uniform(keys[3], (CHANNELS, WINDOWS, 1), jnp.float32, -0.6, 0.6)
    coloured = base[:, :, 2:] + first_tap * base[:, :, 1:-1] + second_tap * base[:, :, :-2]
    amplitude = jnp.exp(jax.random.uniform(keys[4], (CHANNELS, WINDOWS, 1), jnp.float32, 0.0, spread))
    return (amplitude * coloured).astype(jnp.bfloat16)


def draw_partner(key, part):
    players = N_PAIR
    odd_count = N_PAIR - 1
    key_rounds, key_label = jax.random.split(key)
    chosen = jax.random.permutation(key_rounds, odd_count)[:ROUNDS].astype(jnp.int32)
    tag_name = jax.random.permutation(key_label, players).astype(jnp.int32)
    seats = jnp.arange(players, dtype=jnp.int32)
    others = (2 * chosen[:, None] - seats[None, :]) % odd_count
    anchor_pairing = jnp.where(seats[None, :] == chosen[:, None], odd_count, others)
    anchor_pairing = jnp.where(seats[None, :] == odd_count, chosen[:, None], anchor_pairing)
    renamed_tags = tag_name[anchor_pairing]
    final_output = jnp.zeros((ROUNDS, players), jnp.int32)
    pairing_round_rows = jnp.broadcast_to(jnp.arange(ROUNDS, dtype=jnp.int32)[:, None], (ROUNDS, players))
    column_numbers = jnp.broadcast_to(tag_name[None, :], (ROUNDS, players))
    return final_output.at[pairing_round_rows, column_numbers].set(renamed_tags)


def setup_inputs(seed: int = 0) -> dict:
    key_of = jax.random.split(jax.random.key(seed), 4)
    return {
        "traces": draw_traces(jax.random.fold_in(key_of[3], 71), 0),
        "partner": draw_partner(jax.random.fold_in(key_of[3], 71), 0),
        "block_ids": jax.random.permutation(key_of[2], N_PAIR).astype(jnp.int32),
    }


def tapered_table():
    sample = jnp.arange(SAMPLES, dtype=jnp.int32)
    freq = FIRST_BIN + BIN_STEP * jnp.arange(BINS, dtype=jnp.int32)
    phase = sample[:, None] * freq[None, :] % SAMPLES
    angle = 2.0 * math.pi / SAMPLES * phase.astype(jnp.float32)
    taper = 0.5 - 0.5 * jnp.cos(2.0 * math.pi / SAMPLES * sample.astype(jnp.float32))
    real_part = taper[:, None] * jnp.cos(angle)
    imag_part = -taper[:, None] * jnp.sin(angle)
    return jnp.concatenate([real_part, imag_part], axis=1).astype(jnp.bfloat16)

def whitened(trace_rows, dft_table):
    raw = jnp.dot(trace_rows, dft_table, preferred_element_type=jnp.float32)
    power = lax.optimization_barrier(jnp.mean(raw * raw, axis=-1, keepdims=True))
    return (raw * lax.rsqrt(power + 1e-05)).astype(jnp.bfloat16)

def reference(traces, partner, block_ids):
    dft_table = tapered_table()
    blocks = traces.reshape(N_PAIR, BLK * WINDOWS, SAMPLES)
    spectra = lax.map(lambda trace_rows: whitened(trace_rows, dft_table), blocks)
    spectra = spectra.reshape(N_PAIR, BLK, WINDOWS, 2, BINS).transpose(0, 3, 4, 2, 1)
    holder = jnp.argsort(block_ids).astype(jnp.int32)
    local_spec = spectra.astype(jnp.float32)
    rotated = jnp.concatenate([local_spec[:, 1:2], -local_spec[:, 0:1]], axis=1)
    stacked = jnp.stack([local_spec, rotated], axis=1)
    stack_scale = 1.0 / math.sqrt(WINDOWS)
    results = []
    for round_no in range(ROUNDS):
        partner_dev = holder[partner[round_no][block_ids]].astype(jnp.int32)
        remote = spectra[partner_dev].astype(jnp.float32)
        corr = jnp.einsum('nkcbwi,ncbwj->bknij', stacked, remote, precision=lax.Precision.HIGHEST)
        corr = corr * stack_scale
        results.append(corr.reshape(BINS, 2, CHANNELS, BLK))
    return jnp.stack(results, axis=0)
```

```python
import functools
import math

import jax
import jax.numpy as jnp
from jax import lax
from jax.experimental import pallas as pl
from jax.experimental.pallas import tpu as pltpu
from jax.sharding import PartitionSpec as P

SAMPLES = 1024
BINS = 32
FIRST_BIN = 16
BIN_STEP = 8
ROUNDS = 2
LANES = 128
WIN_ROWS = 16
VMEM_BYTES = 40 * 1024 * 1024


def tapered_table(win_count):
    sample = jnp.arange(SAMPLES, dtype=jnp.int32)
    bins_dev = BINS // win_count
    me = lax.axis_index("win")
    owner = me ^ jnp.arange(win_count, dtype=jnp.int32)
    bins = (owner[:, None] * bins_dev + jnp.arange(bins_dev, dtype=jnp.int32)[None, :]).reshape(-1)
    freq = FIRST_BIN + BIN_STEP * bins
    phase = sample[:, None] * freq[None, :] % SAMPLES
    angle = 2.0 * math.pi / SAMPLES * phase.astype(jnp.float32)
    taper = 0.5 - 0.5 * jnp.cos(2.0 * math.pi / SAMPLES * sample.astype(jnp.float32))
    real_part = taper[:, None] * jnp.cos(angle)
    imag_part = -taper[:, None] * jnp.sin(angle)
    both = jnp.stack([real_part, imag_part], axis=2).reshape(SAMPLES, 2 * BINS)
    return both.astype(jnp.bfloat16)


def spectra_kernel(steps, n_out, low_ref, high_ref, table_ref, *rest):
    outs, raw_ref, turned_ref = rest[:n_out], rest[n_out], rest[n_out + 1]
    step = pl.program_id(1)
    rows = low_ref.shape[0] * WIN_ROWS
    low = low_ref[...].reshape(rows, SAMPLES)
    high = high_ref[...].reshape(rows, SAMPLES)
    raw = jnp.dot(low, table_ref[0], preferred_element_type=jnp.float32)
    raw += jnp.dot(high, table_ref[1], preferred_element_type=jnp.float32)
    raw_ref[pl.ds(pl.multiple_of(step * rows, rows), rows), :] = raw

    @pl.when(step == steps - 1)
    def _():
        columns = 2 * BINS
        for w in range(WIN_ROWS):
            turned = raw_ref[pl.ds(w, LANES, stride=WIN_ROWS), :].T
            for half in range(2):
                part = turned[half * columns : (half + 1) * columns]
                power = jnp.mean(part * part, axis=0, keepdims=True)
                first = half * columns * WIN_ROWS + w
                turned_ref[pl.ds(first, columns, stride=WIN_ROWS), :] = part * lax.rsqrt(power + 1e-05)
        per = columns // n_out
        for s in range(n_out):
            for half in range(2):
                first = (half * columns + s * per) * WIN_ROWS
                piece = turned_ref[first : first + per * WIN_ROWS, :].astype(jnp.bfloat16)
                outs[s][:, :, half * LANES : (half + 1) * LANES] = piece.reshape(per, WIN_ROWS, LANES)


def local_spectra(traces, win_count):
    channels, windows, samples = traces.shape
    table = tapered_table(win_count)
    columns = table.shape[1]
    zero = jnp.zeros_like(table)
    tables = jnp.stack([jnp.concatenate([table, zero], 1), jnp.concatenate([zero, table], 1)], 0)
    chan_rows = 16
    steps = channels // 2 // chan_rows
    per = columns // win_count
    block = (chan_rows, WIN_ROWS, samples)
    return pl.pallas_call(
        functools.partial(spectra_kernel, steps, win_count),
        grid=(windows // WIN_ROWS, steps),
        in_specs=[
            pl.BlockSpec(block, lambda w, i: (i, w, 0)),
            pl.BlockSpec(block, lambda w, i: (i + steps, w, 0)),
            pl.BlockSpec((2, samples, 2 * columns), lambda w, i: (0, 0, 0)),
        ],
        out_specs=[pl.BlockSpec((per, WIN_ROWS, channels), lambda w, i: (0, w, 0))] * win_count,
        out_shape=[jax.ShapeDtypeStruct((per, windows, channels), jnp.bfloat16)] * win_count,
        scratch_shapes=[
            pltpu.VMEM((LANES * WIN_ROWS, 2 * columns), jnp.float32),
            pltpu.VMEM((2 * columns * WIN_ROWS, LANES), jnp.float32),
        ],
        compiler_params=pltpu.CompilerParams(vmem_limit_bytes=VMEM_BYTES),
        name="spectra",
    )(traces, traces, tables)


def correlate_kernel(scale, n_chunks, *refs):
    locals_, remotes, out_ref = refs[:n_chunks], refs[n_chunks : 2 * n_chunks], refs[2 * n_chunks]
    bin_no, round_no = pl.program_id(0), pl.program_id(1)
    windows, channels = locals_[0].shape[1:]
    left, right, turned = [], [], []
    for s in range(n_chunks):
        left += [locals_[s][2 * bin_no], locals_[s][2 * bin_no + 1]]
        real, imag = remotes[s][round_no, 2 * bin_no], remotes[s][round_no, 2 * bin_no + 1]
        right += [real, imag]
        turned += [-imag, real]
    left = jnp.concatenate(left, axis=0)
    contract = (((0,), (0,)), ((), ()))
    for part, rows in enumerate((right, turned)):
        product = lax.dot_general(
            left, jnp.concatenate(rows, axis=0), contract, preferred_element_type=jnp.float32
        )
        out_ref[0, 0, part] = product * scale


def correlate(own, remotes, windows):
    n_chunks = len(own)
    channels = own[0].shape[-1]
    bins_dev = own[0].shape[0] // 2
    whole = pl.BlockSpec(memory_space=pltpu.VMEM)
    return pl.pallas_call(
        functools.partial(correlate_kernel, 1.0 / math.sqrt(windows), n_chunks),
        grid=(bins_dev, ROUNDS),
        in_specs=[whole] * (2 * n_chunks),
        out_specs=pl.BlockSpec((1, 1, 2, channels, channels), lambda b, r: (r, b, 0, 0, 0)),
        out_shape=jax.ShapeDtypeStruct((ROUNDS, bins_dev, 2, channels, channels), jnp.float32),
        compiler_params=pltpu.CompilerParams(vmem_limit_bytes=VMEM_BYTES),
        name="cross_spectra",
    )(*own, *remotes)


def partner_positions(partner, block_ids, count):
    slots = jnp.arange(count, dtype=jnp.int32)
    holder = jnp.sum(jnp.where(block_ids[None, :] == slots[:, None], slots[None, :], 0), axis=1)
    at_block = block_ids[:, None] == slots[None, :]
    wanted = jnp.sum(jnp.where(at_block[None], partner[:, None, :], 0), axis=2)
    return jnp.sum(jnp.where(wanted[:, :, None] == slots, holder, 0), axis=2)


def swap(value, axis, distance):
    count = lax.axis_size(axis)
    return lax.ppermute(value, axis, [(i, i ^ distance) for i in range(count)])


def gather_even(piece, pair_count):
    half = piece.shape[0] // 2
    found = {0: (piece[:half], piece[half:])}
    for distance in range(2, pair_count, 2):
        if distance != 6:
            whole = swap(piece, "pair", distance)
            found[distance] = (whole[:half], whole[half:])
    if 6 < pair_count:
        found[6] = (swap(found[4][0], "pair", 2), swap(found[2][1], "pair", 4))
    return found


def pick(found, distance):
    halves = []
    for part in range(2):
        items = sorted(found.items())
        value = items[-1][1][part]
        for at, pieces in items[:-1]:
            value = jnp.where(distance == at, pieces[part], value)
        halves.append(value)
    return jnp.concatenate(halves, axis=0)


def local(traces, partner, block_ids):
    pair_count = lax.axis_size("pair")
    win_count = lax.axis_size("win")
    windows_dev = traces.shape[1]
    me = lax.axis_index("pair")
    slots = jnp.arange(pair_count, dtype=jnp.int32)
    paired = partner_positions(partner, block_ids, pair_count)
    mine = jnp.sum(jnp.where(slots == me, paired, 0), axis=1) ^ me
    beside = jnp.sum(jnp.where(slots == (me ^ 1), paired, 0), axis=1) ^ me
    sent = local_spectra(traces, win_count)
    own = [sent[0]] + [swap(sent[s], "win", s) for s in range(1, win_count)]
    remotes = []
    for piece in own:
        found = gather_even(piece, pair_count)
        outgoing = jnp.stack([pick(found, beside[r]) for r in range(ROUNDS)], axis=0)
        arrived = swap(outgoing, "pair", 1)
        remotes.append(
            jnp.stack(
                [
                    jnp.where(mine[r] % 2 == 1, arrived[r], pick(found, mine[r]))
                    for r in range(ROUNDS)
                ],
                axis=0,
            )
        )
    return correlate(own, remotes, windows_dev * win_count)


def solution(mesh):
    placed = (P("pair", "win", None), P(), P())
    return jax.shard_map(
        local,
        mesh=mesh,
        in_specs=placed,
        out_specs=P(None, "win", None, "pair", None),
        check_vma=False,
    )
```

```python
import functools
import math

import jax
import jax.numpy as jnp
import numpy as np
from jax import lax
from jax.experimental import pallas as pl
from jax.experimental.pallas import tpu as pltpu
from jax.sharding import PartitionSpec as P

BINS = 32
FIRST_BIN = 16
BIN_STEP = 8
ROUNDS = 2
LANES = 128
WIN_ROWS = 16
PITCH = 20
VMEM_BYTES = 44 * 1024 * 1024


def tapered_table(samples):
    sample = np.arange(samples, dtype=np.int32)
    freq = FIRST_BIN + BIN_STEP * np.arange(BINS, dtype=np.int32)
    phase = sample[:, None] * freq[None, :] % samples
    step = np.float32(2.0 * math.pi / samples)
    angle = step * phase.astype(np.float32)
    taper = np.float32(0.5) - np.float32(0.5) * np.cos(step * sample.astype(np.float32))
    both = np.stack([taper[:, None] * np.cos(angle), -taper[:, None] * np.sin(angle)], axis=2)
    both = both.reshape(samples, 2 * BINS)
    zero = np.zeros_like(both)
    tables = np.stack([np.concatenate([both, zero], 1), np.concatenate([zero, both], 1)], 0)
    return jnp.asarray(tables, dtype=jnp.bfloat16)


def spectra_kernel(chan_rows, n_out, win_ref, traces_ref, table_hbm, *rest):
    outs = rest[:n_out]
    raw_ref, turned_ref, traces_buf, table_ref, sems, table_sem = rest[n_out:]
    columns = 2 * BINS
    per = columns // n_out
    samples = traces_ref.shape[2]
    steps = LANES // chan_rows
    halves = traces_ref.shape[1] // WIN_ROWS
    rows = chan_rows * WIN_ROWS

    def copy(h, i, g):
        first = g * LANES + i * chan_rows
        return pltpu.make_async_copy(
            traces_ref.at[pl.ds(first, chan_rows), pl.ds(h * WIN_ROWS, WIN_ROWS), :],
            traces_buf.at[h, pl.ds(first, chan_rows)],
            sems.at[h, i, g],
        )

    table_copy = pltpu.make_async_copy(table_hbm, table_ref, table_sem)
    table_copy.start()
    for h in range(halves):

        @pl.loop(0, steps)
        def _(i):
            copy(h, i, 0).start()
            copy(h, i, 1).start()

    table_copy.wait()
    for h in range(halves):

        @pl.loop(0, steps)
        def _(i):
            copy(h, i, 0).wait()
            copy(h, i, 1).wait()
            low = traces_buf[h, pl.ds(i * chan_rows, chan_rows)].reshape(rows, samples)
            high = traces_buf[h, pl.ds(LANES + i * chan_rows, chan_rows)].reshape(rows, samples)
            raw = jnp.dot(low, table_ref[0], preferred_element_type=jnp.float32)
            raw += jnp.dot(high, table_ref[1], preferred_element_type=jnp.float32)
            base = pl.multiple_of(i * (chan_rows * PITCH), 8)
            for c in range(chan_rows):
                raw_ref[pl.ds(base + c * PITCH, WIN_ROWS), :] = raw[c * WIN_ROWS : (c + 1) * WIN_ROWS]

        for w in range(WIN_ROWS):
            turned = raw_ref[pl.ds(w, LANES, stride=PITCH), :].T
            for g in range(2):
                part = turned[g * columns : (g + 1) * columns]
                power = jnp.mean(part * part, axis=0, keepdims=True)
                first = g * columns * PITCH + w
                turned_ref[pl.ds(first, columns, stride=PITCH), :] = part * lax.rsqrt(power + 1e-05)
        for s in range(n_out):
            base = pl.multiple_of((win_ref[0] ^ s) * (per * PITCH), 8)
            for g in range(2):
                for k in range(per):
                    piece = turned_ref[pl.ds(base + (g * columns + k) * PITCH, WIN_ROWS), :]
                    outs[s][k, h * WIN_ROWS : (h + 1) * WIN_ROWS, g * LANES : (g + 1) * LANES] = (
                        piece.astype(jnp.bfloat16)
                    )


def local_spectra(traces, win_count):
    channels, windows, samples = traces.shape
    columns = 2 * BINS
    chan_rows = 32
    per = columns // win_count
    steps, halves = LANES // chan_rows, windows // WIN_ROWS
    flops = 2 * channels * windows * samples * columns
    return pl.pallas_call(
        functools.partial(spectra_kernel, chan_rows, win_count),
        in_specs=[
            pl.BlockSpec(memory_space=pltpu.SMEM),
            pl.BlockSpec(memory_space=pl.ANY),
            pl.BlockSpec(memory_space=pl.ANY),
        ],
        out_specs=[pl.BlockSpec(memory_space=pltpu.VMEM)] * win_count,
        out_shape=[jax.ShapeDtypeStruct((per, windows, channels), jnp.bfloat16)] * win_count,
        scratch_shapes=[
            pltpu.VMEM((LANES * PITCH, 2 * columns), jnp.float32),
            pltpu.VMEM((2 * columns * PITCH, LANES), jnp.float32),
            pltpu.VMEM((halves, channels, WIN_ROWS, samples), jnp.bfloat16),
            pltpu.VMEM((2, samples, 2 * columns), jnp.bfloat16),
            pltpu.SemaphoreType.DMA((halves, steps, 2)),
            pltpu.SemaphoreType.DMA,
        ],
        compiler_params=pltpu.CompilerParams(vmem_limit_bytes=VMEM_BYTES),
        cost_estimate=pl.CostEstimate(flops=flops, bytes_accessed=traces.size * 2, transcendentals=0),
        name="spectra",
    )(lax.axis_index("win").reshape(1), traces, tapered_table(samples))


def pick_kernel(keys, far_ref, *refs):
    halves, out_ref = refs[:-1], refs[-1]
    half = halves[0].shape[0] // 2
    for r in range(ROUNDS):
        for n, at in enumerate(keys):

            @pl.when(far_ref[r] == at)
            def _():
                low, high = halves[2 * n], halves[2 * n + 1]
                out_ref[r, :half] = low[:half]
                out_ref[r, half:] = high[high.shape[0] - half :]


def pick(found, far):
    keys = sorted(found)
    halves = [h for at in keys for h in found[at]]
    rows, windows, channels = found[0][0].shape
    whole = pl.BlockSpec(memory_space=pltpu.VMEM)
    return pl.pallas_call(
        functools.partial(pick_kernel, keys),
        in_specs=[pl.BlockSpec(memory_space=pltpu.SMEM)] + [whole] * len(halves),
        out_specs=whole,
        out_shape=jax.ShapeDtypeStruct((ROUNDS, rows, windows, channels), jnp.bfloat16),
        compiler_params=pltpu.CompilerParams(vmem_limit_bytes=VMEM_BYTES),
        name="pick",
    )(far, *halves)


def left_kernel(n_chunks, *refs):
    own, out_ref = refs[:n_chunks], refs[n_chunks]
    channels = out_ref.shape[1] // 2

    @pl.loop(0, out_ref.shape[0])
    def _(bin_no):
        straight, turned = [], []
        for s in range(n_chunks):
            real, imag = own[s][2 * bin_no], own[s][2 * bin_no + 1]
            straight += [real, imag]
            turned += [imag, -real]
        out_ref[bin_no, :channels] = jnp.concatenate(straight, axis=0).T
        out_ref[bin_no, channels:] = jnp.concatenate(turned, axis=0).T


def left_side(own, windows):
    rows, _, channels = own[0].shape
    whole = pl.BlockSpec(memory_space=pltpu.VMEM)
    return pl.pallas_call(
        functools.partial(left_kernel, len(own)),
        in_specs=[whole] * len(own),
        out_specs=whole,
        out_shape=jax.ShapeDtypeStruct((rows // 2, 2 * channels, 2 * windows), jnp.bfloat16),
        compiler_params=pltpu.CompilerParams(vmem_limit_bytes=VMEM_BYTES),
        name="left_side",
    )(*own)


def correlate_kernel(scale, n_chunks, keys, far_ref, left_ref, *refs):
    beside, refs = refs[:n_chunks], refs[n_chunks:]
    found, (out_hbm, right_ref, result_ref, sems) = refs[:-4], refs[-4:]
    bins_dev, both, depth = left_ref.shape
    rows, windows, channels = beside[0].shape[1:]
    half = rows // 2
    for r in range(ROUNDS):
        far = far_ref[r]

        @pl.when(far % 2 == 1)
        def _():
            for s in range(n_chunks):
                right_ref[r, s] = beside[s][r]

        for n, at in enumerate(keys):

            @pl.when(far == at)
            def _():
                for s in range(n_chunks):
                    low, high = found[(s * len(keys) + n) * 2 : (s * len(keys) + n) * 2 + 2]
                    right_ref[r, s, :half] = low[:half]
                    right_ref[r, s, half:] = high[high.shape[0] - half :]

    def send(bin_no, r):
        slot = bin_no % 2
        return pltpu.make_async_copy(result_ref.at[slot, r], out_hbm.at[r, bin_no], sems.at[slot, r])

    @pl.loop(0, bins_dev)
    def _(bin_no):
        for r in range(ROUNDS):
            right = jnp.concatenate(
                [right_ref[r, s, 2 * bin_no + part] for s in range(n_chunks) for part in range(2)], axis=0
            )

            @pl.when(bin_no >= 2)
            def _():
                send(bin_no - 2, r).wait()

            for part in range(2):
                left = left_ref[bin_no, part * channels : (part + 1) * channels]
                product = jnp.dot(left, right, preferred_element_type=jnp.float32)
                result_ref[bin_no % 2, r, part] = product * scale
            send(bin_no, r).start()

    for bin_no in range(max(bins_dev - 2, 0), bins_dev):
        for r in range(ROUNDS):
            send(bin_no, r).wait()


def correlate(far, left, beside, found, windows):
    n_chunks = len(beside)
    _, rows, windows_dev, channels = beside[0].shape
    bins_dev = rows // 2
    keys = [at for at in sorted(found[0]) if at]
    halves = [h for pieces in found for at in keys for h in pieces[at]]
    whole = pl.BlockSpec(memory_space=pltpu.VMEM)
    result = (ROUNDS, bins_dev, 2, channels, channels)
    flops = 8 * ROUNDS * bins_dev * windows * channels * channels
    return pl.pallas_call(
        functools.partial(correlate_kernel, 1.0 / math.sqrt(windows), n_chunks, keys),
        in_specs=[pl.BlockSpec(memory_space=pltpu.SMEM)] + [whole] * (1 + n_chunks + len(halves)),
        out_specs=pl.BlockSpec(memory_space=pl.ANY),
        out_shape=jax.ShapeDtypeStruct(result, jnp.float32),
        scratch_shapes=[
            pltpu.VMEM((ROUNDS, n_chunks, rows, windows_dev, channels), jnp.bfloat16),
            pltpu.VMEM((2, ROUNDS, 2, channels, channels), jnp.float32),
            pltpu.SemaphoreType.DMA((2, ROUNDS)),
        ],
        compiler_params=pltpu.CompilerParams(vmem_limit_bytes=VMEM_BYTES),
        cost_estimate=pl.CostEstimate(flops=flops, bytes_accessed=4 * math.prod(result), transcendentals=0),
        name="cross_spectra",
    )(far, left, *beside, *halves)


def partner_positions(partner, block_ids, count):
    slots = jnp.arange(count, dtype=jnp.int32)
    holder = jnp.sum(jnp.where(block_ids[None, :] == slots[:, None], slots[None, :], 0), axis=1)
    at_block = block_ids[:, None] == slots[None, :]
    wanted = jnp.sum(jnp.where(at_block[None], partner[:, None, :], 0), axis=2)
    return jnp.sum(jnp.where(wanted[:, :, None] == slots, holder, 0), axis=2)


def swap(value, axis, distance):
    count = lax.axis_size(axis)
    return lax.ppermute(value, axis, [(i, i ^ distance) for i in range(count)])


def after(value, *others):
    return lax.optimization_barrier((value, *others))[0]


def gather_even(piece, pair_count):
    half = piece.shape[0] // 2
    found = {0: (piece, piece)}
    for distance in range(2, pair_count, 2):
        if distance != 6:
            whole = swap(piece, "pair", distance)
            found[distance] = (whole, whole)
    if 6 < pair_count:
        found[6] = (swap(found[4][0][:half], "pair", 2), swap(found[2][1][half:], "pair", 4))
    return found


def local(traces, partner, block_ids):
    pair_count = lax.axis_size("pair")
    win_count = lax.axis_size("win")
    windows_dev = traces.shape[1]
    me = lax.axis_index("pair")
    slots = jnp.arange(pair_count, dtype=jnp.int32)
    paired = partner_positions(partner, block_ids, pair_count)
    mine = jnp.sum(jnp.where(slots == me, paired, 0), axis=1) ^ me
    beside = jnp.sum(jnp.where(slots == (me ^ 1), paired, 0), axis=1) ^ me
    sent = local_spectra(traces, win_count)
    own = [sent[0]]
    for s in range(1, win_count):
        own.append(swap(after(sent[s], own[2]) if s == 3 else sent[s], "win", s))
    found = []
    for s, piece in enumerate(own):
        direct = [at for at in (2, 4) if at < pair_count]
        if s >= 2:
            piece = after(piece, *[found[s - 1][at][0] for at in direct], *found[s - 2].get(6, ()))
        found.append(gather_even(piece, pair_count))
    arrived = [swap(pick(pieces, beside), "pair", 1) for pieces in found]
    windows = windows_dev * win_count
    return correlate(mine, left_side(own, windows), arrived, found, windows)


def solution(mesh):
    placed = (P("pair", "win", None), P(), P())
    return jax.shard_map(
        local,
        mesh=mesh,
        in_specs=placed,
        out_specs=P(None, "win", None, "pair", None),
        check_vma=False,
    )
```

```python
import functools
import math

import jax
import jax.numpy as jnp
from jax import lax
from jax.experimental import pallas as pl
from jax.experimental.pallas import tpu as pltpu
from jax.sharding import PartitionSpec as P

BINS = 32
FIRST_BIN = 16
BIN_STEP = 8
ROUNDS = 2
LANES = 128
WIN_ROWS = 16
PITCH = 20
VMEM_BYTES = 44 * 1024 * 1024


def fill_table(table_ref):
    samples, columns = table_ref.shape[1], 2 * BINS
    period = samples // math.gcd(FIRST_BIN, BIN_STEP, samples)
    step = 2.0 * math.pi / samples
    sample = lax.broadcasted_iota(jnp.int32, (period, LANES), 0)
    column = lax.broadcasted_iota(jnp.int32, (period, LANES), 1) & (columns - 1)
    freq = FIRST_BIN + BIN_STEP * (column >> 1)
    angle = step * ((sample * freq) & (samples - 1)).astype(jnp.float32)
    waves = jnp.where((column & 1) == 0, jnp.cos(angle), -jnp.sin(angle))
    around = step * sample.astype(jnp.float32)
    cosine, sine = jnp.cos(around), jnp.sin(around)
    low = lax.broadcasted_iota(jnp.int32, (period, LANES), 1) < columns
    for n in range(samples // period):
        turn = 2.0 * math.pi * n * period / samples
        taper = 0.5 - 0.5 * (math.cos(turn) * cosine - math.sin(turn) * sine)
        tapered = taper * waves
        rows = slice(n * period, (n + 1) * period)
        table_ref[0, rows] = jnp.where(low, tapered, 0.0).astype(jnp.bfloat16)
        table_ref[1, rows] = jnp.where(low, 0.0, tapered).astype(jnp.bfloat16)


def spectra_kernel(chan_rows, win_count, pieces, win_ref, traces_ref, *rest):
    outs = rest[: len(pieces)]
    raw_ref, turned_ref, traces_buf, table_ref, sems = rest[len(pieces) :]
    columns = 2 * BINS
    per = columns // win_count
    samples = traces_ref.shape[2]
    steps = LANES // chan_rows
    halves = traces_ref.shape[1] // WIN_ROWS
    rows = chan_rows * WIN_ROWS

    def copy(h, i, g):
        first = g * LANES + i * chan_rows
        return pltpu.make_async_copy(
            traces_ref.at[pl.ds(first, chan_rows), pl.ds(h * WIN_ROWS, WIN_ROWS), :],
            traces_buf.at[h, pl.ds(first, chan_rows)],
            sems.at[h, i, g],
        )

    for h in range(halves):

        @pl.loop(0, steps)
        def _(i):
            copy(h, i, 0).start()
            copy(h, i, 1).start()

    fill_table(table_ref)
    for h in range(halves):

        @pl.loop(0, steps)
        def _(i):
            copy(h, i, 0).wait()
            copy(h, i, 1).wait()
            low = traces_buf[h, pl.ds(i * chan_rows, chan_rows)].reshape(rows, samples)
            high = traces_buf[h, pl.ds(LANES + i * chan_rows, chan_rows)].reshape(rows, samples)
            raw = jnp.dot(low, table_ref[0], preferred_element_type=jnp.float32)
            raw += jnp.dot(high, table_ref[1], preferred_element_type=jnp.float32)
            base = pl.multiple_of(i * (chan_rows * PITCH), 8)
            for c in range(chan_rows):
                raw_ref[pl.ds(base + c * PITCH, WIN_ROWS), :] = raw[c * WIN_ROWS : (c + 1) * WIN_ROWS]

        for w in range(WIN_ROWS):
            turned = raw_ref[pl.ds(w, LANES, stride=PITCH), :].T
            for g in range(2):
                part = turned[g * columns : (g + 1) * columns]
                power = jnp.mean(part * part, axis=0, keepdims=True)
                first = g * columns * PITCH + w
                turned_ref[pl.ds(first, columns, stride=PITCH), :] = part * lax.rsqrt(power + 1e-05)
        for out_ref, (s, low, high) in zip(outs, pieces):
            base = pl.multiple_of((win_ref[0] ^ s) * (per * PITCH), 8)
            for g in range(2):
                for k in range(low, high):
                    taken = turned_ref[pl.ds(base + (g * columns + k) * PITCH, WIN_ROWS), :]
                    out_ref[k - low, h * WIN_ROWS : (h + 1) * WIN_ROWS, g * LANES : (g + 1) * LANES] = (
                        taken.astype(jnp.bfloat16)
                    )


def local_spectra(traces, win_count, pieces):
    channels, windows, samples = traces.shape
    columns = 2 * BINS
    chan_rows = 32
    steps, halves = LANES // chan_rows, windows // WIN_ROWS
    flops = 2 * channels * windows * samples * columns
    return pl.pallas_call(
        functools.partial(spectra_kernel, chan_rows, win_count, pieces),
        in_specs=[
            pl.BlockSpec(memory_space=pltpu.SMEM),
            pl.BlockSpec(memory_space=pl.ANY),
        ],
        out_specs=[pl.BlockSpec(memory_space=pltpu.VMEM)] * len(pieces),
        out_shape=[
            jax.ShapeDtypeStruct((high - low, windows, channels), jnp.bfloat16) for _, low, high in pieces
        ],
        scratch_shapes=[
            pltpu.VMEM((LANES * PITCH, 2 * columns), jnp.float32),
            pltpu.VMEM((2 * columns * PITCH, LANES), jnp.float32),
            pltpu.VMEM((halves, channels, WIN_ROWS, samples), jnp.bfloat16),
            pltpu.VMEM((2, samples, 2 * columns), jnp.bfloat16),
            pltpu.SemaphoreType.DMA((halves, steps, 2)),
        ],
        compiler_params=pltpu.CompilerParams(vmem_limit_bytes=VMEM_BYTES),
        cost_estimate=pl.CostEstimate(flops=flops, bytes_accessed=traces.size * 2, transcendentals=0),
        name="spectra",
    )(lax.axis_index("win").reshape(1), traces)


def cut(found, low, high):
    cuts = {}
    for at, parts in found.items():
        cuts[at], start = [], 0
        for part in parts:
            first, last = max(low, start), min(high, start + part.shape[0])
            if first < last:
                cuts[at].append((part, first - start, last - first))
            start += part.shape[0]
    return cuts


def pick_kernel(places, far_ref, *refs):
    out_ref = refs[-1]
    for r in range(ROUNDS):
        for at in places:

            @pl.when(far_ref[r] == at)
            def _():
                row = 0
                for n, first, count in places[at]:
                    out_ref[r, row : row + count] = refs[n][first : first + count]
                    row += count


def pick(cuts, far):
    arrays, places = [], {at: [] for at in sorted(cuts[0])}
    for chunk in cuts:
        for at in places:
            for part, first, count in chunk[at]:
                places[at].append((len(arrays), first, count))
                arrays.append(part)
    rows = sum(count for _, _, count in places[0])
    whole = pl.BlockSpec(memory_space=pltpu.VMEM)
    return pl.pallas_call(
        functools.partial(pick_kernel, places),
        in_specs=[pl.BlockSpec(memory_space=pltpu.SMEM)] + [whole] * len(arrays),
        out_specs=whole,
        out_shape=jax.ShapeDtypeStruct((ROUNDS, rows, *arrays[0].shape[1:]), jnp.bfloat16),
        compiler_params=pltpu.CompilerParams(vmem_limit_bytes=VMEM_BYTES),
        name="pick",
    )(far, *arrays)


def left_kernel(*refs):
    own, out_ref = refs[:-1], refs[-1]
    channels = out_ref.shape[1] // 2

    @pl.loop(0, out_ref.shape[0])
    def _(bin_no):
        straight, turned = [], []
        for source in own:
            real, imag = source[2 * bin_no], source[2 * bin_no + 1]
            straight += [real, imag]
            turned += [imag, -real]
        out_ref[bin_no, :channels] = jnp.concatenate(straight, axis=0).T
        out_ref[bin_no, channels:] = jnp.concatenate(turned, axis=0).T


def left_side(own, windows):
    rows, _, channels = own[0].shape
    whole = pl.BlockSpec(memory_space=pltpu.VMEM)
    return pl.pallas_call(
        left_kernel,
        in_specs=[whole] * len(own),
        out_specs=whole,
        out_shape=jax.ShapeDtypeStruct((rows // 2, 2 * channels, 2 * windows), jnp.bfloat16),
        compiler_params=pltpu.CompilerParams(vmem_limit_bytes=VMEM_BYTES),
        name="left_side",
    )(*own)


def correlate_kernel(scale, first_bin, layout, far_ref, left_ref, *refs):
    out_hbm, right_ref, result_ref, sems = refs[-4:]
    bins, _, _, channels, _ = result_ref.shape
    rows = right_ref.shape[2]
    for r in range(ROUNDS):
        far = far_ref[r]

        @pl.when(far % 2 == 1)
        def _():
            for c, ((n, first), _) in enumerate(layout):
                right_ref[r, c] = refs[n][r, first : first + rows]

        for at in layout[0][1]:

            @pl.when(far == at)
            def _():
                for c, (_, by_key) in enumerate(layout):
                    row = 0
                    for n, first, count in by_key[at]:
                        right_ref[r, c, row : row + count] = refs[n][first : first + count]
                        row += count

    def send(bin_no, r):
        target = out_hbm.at[r, first_bin + bin_no]
        return pltpu.make_async_copy(result_ref.at[bin_no, r], target, sems.at[bin_no, r])

    @pl.loop(0, bins)
    def _(bin_no):
        for r in range(ROUNDS):
            right = jnp.concatenate(
                [right_ref[r, c, 2 * bin_no + part] for c in range(len(layout)) for part in range(2)], axis=0
            )
            product = jnp.dot(left_ref[first_bin + bin_no], right, preferred_element_type=jnp.float32)
            result_ref[bin_no, r] = (product * scale).reshape(2, channels, channels)
            send(bin_no, r).start()

    @pl.loop(0, bins)
    def _(bin_no):
        for r in range(ROUNDS):
            send(bin_no, r).wait()


def correlate(far, left, other, found, first_bin, bins, result):
    bins_dev, both, depth = left.shape
    channels = both // 2
    low, high = 2 * first_bin, 2 * (first_bin + bins)
    arrays, layout = [], []

    def cover(parts):
        taken, start = [], 0
        for part in parts:
            stop = start + part.shape[0]
            first, last = max(low, start), min(high, stop)
            if first < last:
                taken.append((len(arrays), first - start, last - first))
                arrays.append(part)
            start = stop
        return taken

    across = [array for array, _ in other]
    kept = [n for n, array in enumerate(across) if not any(array is seen for seen in across[:n])]
    arrays += [across[n] for n in kept]
    for chunk, (array, first) in zip(found, other):
        n = [array is across[m] for m in kept].index(True)
        layout.append(((n, first), {at: cover(chunk[at]) for at in sorted(chunk) if at}))
    windows_dev = found[0][0][0].shape[1]
    before = [] if result is None else [result]
    whole = pl.BlockSpec(memory_space=pltpu.VMEM)
    shape = (ROUNDS, bins_dev, 2, channels, channels)
    flops = 4 * ROUNDS * bins * depth * channels * channels
    bytes_out = 4 * ROUNDS * bins * 2 * channels * channels
    scale = 1.0 / math.sqrt(depth // 2)

    return pl.pallas_call(
        functools.partial(correlate_kernel, scale, first_bin, layout),
        in_specs=[pl.BlockSpec(memory_space=pltpu.SMEM)]
        + [whole] * (1 + len(arrays))
        + [pl.BlockSpec(memory_space=pl.ANY)] * len(before),
        out_specs=pl.BlockSpec(memory_space=pl.ANY),
        out_shape=jax.ShapeDtypeStruct(shape, jnp.float32),
        scratch_shapes=[
            pltpu.VMEM((ROUNDS, len(layout), 2 * bins, windows_dev, channels), jnp.bfloat16),
            pltpu.VMEM((bins, ROUNDS, 2, channels, channels), jnp.float32),
            pltpu.SemaphoreType.DMA((bins, ROUNDS)),
        ],
        input_output_aliases={2 + len(arrays): 0} if before else {},
        compiler_params=pltpu.CompilerParams(vmem_limit_bytes=VMEM_BYTES),
        cost_estimate=pl.CostEstimate(flops=flops, bytes_accessed=bytes_out, transcendentals=0),
        name="cross_spectra",
    )(far, left, *arrays, *before)


def partner_positions(partner, block_ids, count):
    slots = jnp.arange(count, dtype=jnp.int32)
    holder = jnp.sum(jnp.where(block_ids[None, :] == slots[:, None], slots[None, :], 0), axis=1)
    at_block = block_ids[:, None] == slots[None, :]
    wanted = jnp.sum(jnp.where(at_block[None], partner[:, None, :], 0), axis=2)
    return jnp.sum(jnp.where(wanted[:, :, None] == slots, holder, 0), axis=2)


def swap(value, axis, distance):
    count = lax.axis_size(axis)
    return lax.ppermute(value, axis, [(i, i ^ distance) for i in range(count)])


def after(value, *others):
    return lax.optimization_barrier((value, *others))[0] if others else value


def gather_even(piece):
    pair_count = lax.axis_size("pair")
    half = piece.shape[0] // 2
    found = {0: [piece]}
    for distance in range(2, pair_count, 2):
        if distance != 6:
            found[distance] = [swap(piece, "pair", distance)]
    if 6 < pair_count:
        found[6] = [swap(found[4][0][:half], "pair", 2), swap(found[2][0][half:], "pair", 4)]
    return found


def local(traces, partner, block_ids):
    pair_count = lax.axis_size("pair")
    win_count = lax.axis_size("win")
    rows = 2 * BINS // win_count
    windows = traces.shape[1] * win_count
    me = lax.axis_index("pair")
    slots = jnp.arange(pair_count, dtype=jnp.int32)
    paired = partner_positions(partner, block_ids, pair_count)
    mine = jnp.sum(jnp.where(slots == me, paired, 0), axis=1) ^ me
    beside = jnp.sum(jnp.where(slots == (me ^ 1), paired, 0), axis=1) ^ me

    sent = local_spectra(traces, win_count, [(s, 0, rows) for s in range(win_count)])
    own, found = [], []
    for s, piece in enumerate(sent):
        if s:
            piece = swap(after(piece, own[2]) if s == 3 else piece, "win", s)
        own.append(piece)
    for s, piece in enumerate(own):
        if s >= 2:
            near = [part for at in (2, 4) for part in found[s - 1].get(at, [])]
            piece = after(piece, *near, *found[s - 2].get(6, []))
        found.append(gather_even(piece))
    left = left_side(own, windows)
    half, bins = rows // 2, rows // 2
    waited = after(beside, left)
    early = [swap(pick([cut(chunk, 0, rows)], waited), "pair", 1) for chunk in found[:-2]]
    late = [
        swap(pick([cut(chunk, at, at + half) for chunk in found[-2:]], beside), "pair", 1)
        for at in (0, half)
    ]
    result = None
    for part, (low, count) in enumerate(((0, bins // 2), (bins // 2, bins - bins // 2))):
        other = [(array, 2 * low) for array in early] + [(late[part], 0), (late[part], half)]
        result = correlate(mine, left, other, found, low, count, result)
    return result


def solution(mesh):
    placed = (P("pair", "win", None), P(), P())
    return jax.shard_map(
        local,
        mesh=mesh,
        in_specs=placed,
        out_specs=P(None, "win", None, "pair", None),
        check_vma=False,
    )
```

```python
import functools
import math

import jax
import jax.numpy as jnp
from jax import lax
from jax.experimental import pallas as pl
from jax.experimental.pallas import tpu as pltpu
from jax.sharding import PartitionSpec as P

BINS = 32
FIRST_BIN = 16
BIN_STEP = 8
ROUNDS = 2
LANES = 128
WIN_ROWS = 16
PITCH = 20
VMEM_BYTES = 44 * 1024 * 1024


def fill_table(table_ref):
    samples, columns = table_ref.shape[1], 2 * BINS
    period = samples // math.gcd(FIRST_BIN, BIN_STEP, samples)
    step = 2.0 * math.pi / samples
    sample = lax.broadcasted_iota(jnp.int32, (period, LANES), 0)
    column = lax.broadcasted_iota(jnp.int32, (period, LANES), 1) & (columns - 1)
    freq = FIRST_BIN + BIN_STEP * (column >> 1)
    angle = step * ((sample * freq) & (samples - 1)).astype(jnp.float32)
    waves = jnp.where((column & 1) == 0, jnp.cos(angle), -jnp.sin(angle))
    around = step * sample.astype(jnp.float32)
    cosine, sine = jnp.cos(around), jnp.sin(around)
    low = lax.broadcasted_iota(jnp.int32, (period, LANES), 1) < columns
    for n in range(samples // period):
        turn = 2.0 * math.pi * n * period / samples
        taper = 0.5 - 0.5 * (math.cos(turn) * cosine - math.sin(turn) * sine)
        tapered = taper * waves
        rows = slice(n * period, (n + 1) * period)
        table_ref[0, rows] = jnp.where(low, tapered, 0.0).astype(jnp.bfloat16)
        table_ref[1, rows] = jnp.where(low, 0.0, tapered).astype(jnp.bfloat16)


def spectra_kernel(chan_rows, win_count, pieces, win_ref, traces_ref, *rest):
    outs = rest[: len(pieces)]
    raw_ref, turned_ref, traces_buf, table_ref, sems = rest[len(pieces) :]
    columns = 2 * BINS
    per = columns // win_count
    samples = traces_ref.shape[2]
    steps = LANES // chan_rows
    halves = traces_ref.shape[1] // WIN_ROWS
    rows = chan_rows * WIN_ROWS

    def copy(h, i, g):
        first = g * LANES + i * chan_rows
        return pltpu.make_async_copy(
            traces_ref.at[pl.ds(first, chan_rows), pl.ds(h * WIN_ROWS, WIN_ROWS), :],
            traces_buf.at[h, pl.ds(first, chan_rows)],
            sems.at[h, i, g],
        )

    for h in range(halves):

        @pl.loop(0, steps)
        def _(i):
            copy(h, i, 0).start()
            copy(h, i, 1).start()

    fill_table(table_ref)
    for h in range(halves):

        @pl.loop(0, steps)
        def _(i):
            copy(h, i, 0).wait()
            copy(h, i, 1).wait()
            low = traces_buf[h, pl.ds(i * chan_rows, chan_rows)].reshape(rows, samples)
            high = traces_buf[h, pl.ds(LANES + i * chan_rows, chan_rows)].reshape(rows, samples)
            raw = jnp.dot(low, table_ref[0], preferred_element_type=jnp.float32)
            raw += jnp.dot(high, table_ref[1], preferred_element_type=jnp.float32)
            base = pl.multiple_of(i * (chan_rows * PITCH), 8)
            for c in range(chan_rows):
                raw_ref[pl.ds(base + c * PITCH, WIN_ROWS), :] = raw[c * WIN_ROWS : (c + 1) * WIN_ROWS]

        for w in range(WIN_ROWS):
            turned = raw_ref[pl.ds(w, LANES, stride=PITCH), :].T
            for g in range(2):
                part = turned[g * columns : (g + 1) * columns]
                power = jnp.mean(part * part, axis=0, keepdims=True)
                first = g * columns * PITCH + w
                turned_ref[pl.ds(first, columns, stride=PITCH), :] = part * lax.rsqrt(power + 1e-05)
        for out_ref, (s, low, high) in zip(outs, pieces):
            base = pl.multiple_of((win_ref[0] ^ s) * (per * PITCH), 8)
            for g in range(2):
                for k in range(low, high):
                    taken = turned_ref[pl.ds(base + (g * columns + k) * PITCH, WIN_ROWS), :]
                    out_ref[k - low, h * WIN_ROWS : (h + 1) * WIN_ROWS, g * LANES : (g + 1) * LANES] = (
                        taken.astype(jnp.bfloat16)
                    )


def local_spectra(traces, win_count, pieces):
    channels, windows, samples = traces.shape
    columns = 2 * BINS
    chan_rows = 32
    steps, halves = LANES // chan_rows, windows // WIN_ROWS
    flops = 2 * channels * windows * samples * columns
    return pl.pallas_call(
        functools.partial(spectra_kernel, chan_rows, win_count, pieces),
        in_specs=[
            pl.BlockSpec(memory_space=pltpu.SMEM),
            pl.BlockSpec(memory_space=pl.ANY),
        ],
        out_specs=[pl.BlockSpec(memory_space=pltpu.VMEM)] * len(pieces),
        out_shape=[
            jax.ShapeDtypeStruct((high - low, windows, channels), jnp.bfloat16) for _, low, high in pieces
        ],
        scratch_shapes=[
            pltpu.VMEM((LANES * PITCH, 2 * columns), jnp.float32),
            pltpu.VMEM((2 * columns * PITCH, LANES), jnp.float32),
            pltpu.VMEM((halves, channels, WIN_ROWS, samples), jnp.bfloat16),
            pltpu.VMEM((2, samples, 2 * columns), jnp.bfloat16),
            pltpu.SemaphoreType.DMA((halves, steps, 2)),
        ],
        compiler_params=pltpu.CompilerParams(vmem_limit_bytes=VMEM_BYTES),
        cost_estimate=pl.CostEstimate(flops=flops, bytes_accessed=traces.size * 2, transcendentals=0),
        name="spectra",
    )(lax.axis_index("win").reshape(1), traces)


def cut(found, low, high):
    cuts = {}
    for at, parts in found.items():
        cuts[at], start = [], 0
        for part in parts:
            first, last = max(low, start), min(high, start + part.shape[0])
            if first < last:
                cuts[at].append((part, first - start, last - first))
            start += part.shape[0]
    return cuts


def pick_kernel(places, far_ref, *refs):
    out_ref = refs[-1]
    for r in range(ROUNDS):
        for at in places:

            @pl.when(far_ref[r] == at)
            def _():
                row = 0
                for n, first, count in places[at]:
                    out_ref[r, row : row + count] = refs[n][first : first + count]
                    row += count


def pick(cuts, far):
    arrays, places = [], {at: [] for at in sorted(cuts[0])}
    for chunk in cuts:
        for at in places:
            for part, first, count in chunk[at]:
                places[at].append((len(arrays), first, count))
                arrays.append(part)
    rows = sum(count for _, _, count in places[0])
    whole = pl.BlockSpec(memory_space=pltpu.VMEM)
    return pl.pallas_call(
        functools.partial(pick_kernel, places),
        in_specs=[pl.BlockSpec(memory_space=pltpu.SMEM)] + [whole] * len(arrays),
        out_specs=whole,
        out_shape=jax.ShapeDtypeStruct((ROUNDS, rows, *arrays[0].shape[1:]), jnp.bfloat16),
        compiler_params=pltpu.CompilerParams(vmem_limit_bytes=VMEM_BYTES),
        name="pick",
    )(far, *arrays)


def left_kernel(*refs):
    own, out_ref = refs[:-1], refs[-1]
    channels = out_ref.shape[1] // 2

    @pl.loop(0, out_ref.shape[0])
    def _(bin_no):
        straight, turned = [], []
        for source in own:
            real, imag = source[2 * bin_no], source[2 * bin_no + 1]
            straight += [real, imag]
            turned += [imag, -real]
        out_ref[bin_no, :channels] = jnp.concatenate(straight, axis=0).T
        out_ref[bin_no, channels:] = jnp.concatenate(turned, axis=0).T


def left_side(own, windows):
    rows, _, channels = own[0].shape
    whole = pl.BlockSpec(memory_space=pltpu.VMEM)
    return pl.pallas_call(
        left_kernel,
        in_specs=[whole] * len(own),
        out_specs=whole,
        out_shape=jax.ShapeDtypeStruct((rows // 2, 2 * channels, 2 * windows), jnp.bfloat16),
        compiler_params=pltpu.CompilerParams(vmem_limit_bytes=VMEM_BYTES),
        name="left_side",
    )(*own)


def correlate_kernel(scale, layout, far_ref, left_ref, *refs):
    out_hbm, right_ref, result_ref, sems = refs[-4:]
    bins, _, _, channels, _ = result_ref.shape

    for r in range(ROUNDS):
        far = far_ref[r]

        @pl.when(far % 2 == 1)
        def _():
            for c, (across, _) in enumerate(layout):
                row = 0
                for n, first, count in across:
                    right_ref[r, c, row : row + count] = refs[n][r, first : first + count]
                    row += count

        for at in layout[0][1]:

            @pl.when(far == at)
            def _():
                for c, (_, by_key) in enumerate(layout):
                    row = 0
                    for n in by_key[at]:
                        count = refs[n].shape[0]
                        right_ref[r, c, row : row + count] = refs[n][...]
                        row += count

    def send(bin_no, r):
        return pltpu.make_async_copy(result_ref.at[bin_no, r], out_hbm.at[r, bin_no], sems.at[bin_no, r])

    @pl.loop(0, bins)
    def _(bin_no):
        for r in range(ROUNDS):
            right = jnp.concatenate(
                [right_ref[r, c, 2 * bin_no + part] for c in range(len(layout)) for part in range(2)], axis=0
            )
            product = jnp.dot(left_ref[bin_no], right, preferred_element_type=jnp.float32)
            result_ref[bin_no, r] = (product * scale).reshape(2, channels, channels)
            send(bin_no, r).start()

    @pl.loop(0, bins)
    def _(bin_no):
        for r in range(ROUNDS):
            send(bin_no, r).wait()


def correlate(far, left, found, across, other):
    bins, both, depth = left.shape
    channels = both // 2
    arrays, layout = list(across), []

    def numbered(parts):
        arrays.extend(parts)
        return list(range(len(arrays) - len(parts), len(arrays)))

    for chunk, parts in zip(found, other):
        layout.append((parts, {at: numbered(chunk[at]) for at in sorted(chunk) if at}))
    rows, windows_dev, _ = found[0][0][0].shape
    whole = pl.BlockSpec(memory_space=pltpu.VMEM)
    shape = (ROUNDS, bins, 2, channels, channels)
    flops = 4 * ROUNDS * bins * depth * channels * channels
    scale = 1.0 / math.sqrt(depth // 2)
    return pl.pallas_call(
        functools.partial(correlate_kernel, scale, layout),
        in_specs=[pl.BlockSpec(memory_space=pltpu.SMEM)] + [whole] * (1 + len(arrays)),
        out_specs=pl.BlockSpec(memory_space=pl.ANY),
        out_shape=jax.ShapeDtypeStruct(shape, jnp.float32),
        scratch_shapes=[
            pltpu.VMEM((ROUNDS, len(layout), rows, windows_dev, channels), jnp.bfloat16),
            pltpu.VMEM((bins, ROUNDS, 2, channels, channels), jnp.float32),
            pltpu.SemaphoreType.DMA((bins, ROUNDS)),
        ],
        compiler_params=pltpu.CompilerParams(vmem_limit_bytes=VMEM_BYTES),
        cost_estimate=pl.CostEstimate(flops=flops, bytes_accessed=4 * math.prod(shape), transcendentals=0),
        name="cross_spectra",
    )(far, left, *arrays)


def partner_positions(partner, block_ids, count):
    slots = jnp.arange(count, dtype=jnp.int32)
    holder = jnp.sum(jnp.where(block_ids[None, :] == slots[:, None], slots[None, :], 0), axis=1)
    at_block = block_ids[:, None] == slots[None, :]
    wanted = jnp.sum(jnp.where(at_block[None], partner[:, None, :], 0), axis=2)
    return jnp.sum(jnp.where(wanted[:, :, None] == slots, holder, 0), axis=2)


def swap(value, axis, distance):
    count = lax.axis_size(axis)
    return lax.ppermute(value, axis, [(i, i ^ distance) for i in range(count)])


def after(value, *others):
    return lax.optimization_barrier((value, *others))[0] if others else value


def gather_even(piece, relay):
    pair_count = lax.axis_size("pair")
    half = piece.shape[0] // 2
    found = {0: [piece]}
    for distance in range(2, pair_count, 2):
        if distance != 6 or not relay:
            found[distance] = [swap(piece, "pair", distance)]
    if relay and 6 < pair_count:
        found[6] = [swap(found[4][0][:half], "pair", 2), swap(found[2][0][half:], "pair", 4)]
    return found


def local(traces, partner, block_ids):
    pair_count = lax.axis_size("pair")
    win_count = lax.axis_size("win")
    rows = 2 * BINS // win_count
    windows = traces.shape[1] * win_count
    me = lax.axis_index("pair")
    slots = jnp.arange(pair_count, dtype=jnp.int32)
    paired = partner_positions(partner, block_ids, pair_count)
    mine = jnp.sum(jnp.where(slots == me, paired, 0), axis=1) ^ me
    beside = jnp.sum(jnp.where(slots == (me ^ 1), paired, 0), axis=1) ^ me

    sent = local_spectra(traces, win_count, [(s, 0, rows) for s in range(win_count)])
    own, found = [], []
    for s, piece in enumerate(sent):
        if s:
            piece = swap(after(piece, own[2]) if s == 3 else piece, "win", s)
        own.append(piece)
    for s, piece in enumerate(own):
        if s >= 1:
            near = [part for at in (2, 4) for part in found[s - 1].get(at, [])]
            piece = after(piece, *near, *(found[s - 2].get(6, []) if s > 1 else []))
        found.append(gather_even(piece, relay=s > 0))
    left = left_side(own, windows)
    half = rows // 2
    early = [swap(pick([cut(chunk, 0, rows)], beside), "pair", 1) for chunk in found[:-2]]
    late = [
        swap(pick([cut(chunk, at, at + half) for chunk in found[-2:]], beside), "pair", 1)
        for at in (0, half)
    ]
    other = [[(n, 0, rows)] for n in range(len(early))]
    for n in range(2):
        other.append([(len(early) + part, n * half, half) for part in range(2)])
    return correlate(mine, left, found, early + late, other)


def solution(mesh):
    placed = (P("pair", "win", None), P(), P())
    return jax.shard_map(
        local,
        mesh=mesh,
        in_specs=placed,
        out_specs=P(None, "win", None, "pair", None),
        check_vma=False,
    )
```

```python
import functools
import math

import jax
import jax.numpy as jnp
from jax import lax
from jax.experimental import pallas as pl
from jax.experimental.pallas import tpu as pltpu
from jax.sharding import PartitionSpec as P

BINS = 32
FIRST_BIN = 16
BIN_STEP = 8
ROUNDS = 2
LANES = 128
WIN_ROWS = 16
PITCH = 20
VMEM_BYTES = 44 * 1024 * 1024


def fill_table(table_ref):
    samples, columns = table_ref.shape[1], 2 * BINS
    period = samples // math.gcd(FIRST_BIN, BIN_STEP, samples)
    step = 2.0 * math.pi / samples
    sample = lax.broadcasted_iota(jnp.int32, (period, LANES), 0)
    column = lax.broadcasted_iota(jnp.int32, (period, LANES), 1) & (columns - 1)
    freq = FIRST_BIN + BIN_STEP * (column >> 1)
    angle = step * ((sample * freq) & (samples - 1)).astype(jnp.float32)
    waves = jnp.where((column & 1) == 0, jnp.cos(angle), -jnp.sin(angle))
    around = step * sample.astype(jnp.float32)
    cosine, sine = jnp.cos(around), jnp.sin(around)
    low = lax.broadcasted_iota(jnp.int32, (period, LANES), 1) < columns
    for n in range(samples // period):
        turn = 2.0 * math.pi * n * period / samples
        taper = 0.5 - 0.5 * (math.cos(turn) * cosine - math.sin(turn) * sine)
        tapered = taper * waves
        rows = slice(n * period, (n + 1) * period)
        table_ref[0, rows] = jnp.where(low, tapered, 0.0).astype(jnp.bfloat16)
        table_ref[1, rows] = jnp.where(low, 0.0, tapered).astype(jnp.bfloat16)


def spectra_kernel(chan_rows, win_count, pieces, win_ref, traces_ref, *rest):
    outs = rest[: len(pieces)]
    raw_ref, turned_ref, traces_buf, table_ref, sems = rest[len(pieces) :]
    columns = 2 * BINS
    per = columns // win_count
    samples = traces_ref.shape[2]
    steps = LANES // chan_rows
    halves = traces_ref.shape[1] // WIN_ROWS
    rows = chan_rows * WIN_ROWS

    def copy(h, i, g):
        first = g * LANES + i * chan_rows
        return pltpu.make_async_copy(
            traces_ref.at[pl.ds(first, chan_rows), pl.ds(h * WIN_ROWS, WIN_ROWS), :],
            traces_buf.at[h, pl.ds(first, chan_rows)],
            sems.at[h, i, g],
        )

    for h in range(halves):

        @pl.loop(0, steps)
        def _(i):
            copy(h, i, 0).start()
            copy(h, i, 1).start()

    fill_table(table_ref)
    for h in range(halves):

        @pl.loop(0, steps)
        def _(i):
            copy(h, i, 0).wait()
            copy(h, i, 1).wait()
            low = traces_buf[h, pl.ds(i * chan_rows, chan_rows)].reshape(rows, samples)
            high = traces_buf[h, pl.ds(LANES + i * chan_rows, chan_rows)].reshape(rows, samples)
            raw = jnp.dot(low, table_ref[0], preferred_element_type=jnp.float32)
            raw += jnp.dot(high, table_ref[1], preferred_element_type=jnp.float32)
            base = pl.multiple_of(i * (chan_rows * PITCH), 8)
            for c in range(chan_rows):
                raw_ref[pl.ds(base + c * PITCH, WIN_ROWS), :] = raw[c * WIN_ROWS : (c + 1) * WIN_ROWS]

        for w in range(WIN_ROWS):
            turned = raw_ref[pl.ds(w, LANES, stride=PITCH), :].T
            for g in range(2):
                part = turned[g * columns : (g + 1) * columns]
                power = jnp.mean(part * part, axis=0, keepdims=True)
                first = g * columns * PITCH + w
                turned_ref[pl.ds(first, columns, stride=PITCH), :] = part * lax.rsqrt(power + 1e-05)
        for out_ref, (s, low, high) in zip(outs, pieces):
            base = pl.multiple_of((win_ref[0] ^ s) * (per * PITCH), 8)
            for g in range(2):
                for k in range(low, high):
                    taken = turned_ref[pl.ds(base + (g * columns + k) * PITCH, WIN_ROWS), :]
                    out_ref[k - low, h * WIN_ROWS : (h + 1) * WIN_ROWS, g * LANES : (g + 1) * LANES] = (
                        taken.astype(jnp.bfloat16)
                    )


def local_spectra(traces, win_count, pieces):
    channels, windows, samples = traces.shape
    columns = 2 * BINS
    chan_rows = 32
    steps, halves = LANES // chan_rows, windows // WIN_ROWS
    flops = 2 * channels * windows * samples * columns
    return pl.pallas_call(
        functools.partial(spectra_kernel, chan_rows, win_count, pieces),
        in_specs=[
            pl.BlockSpec(memory_space=pltpu.SMEM),
            pl.BlockSpec(memory_space=pl.ANY),
        ],
        out_specs=[pl.BlockSpec(memory_space=pltpu.VMEM)] * len(pieces),
        out_shape=[
            jax.ShapeDtypeStruct((high - low, windows, channels), jnp.bfloat16) for _, low, high in pieces
        ],
        scratch_shapes=[
            pltpu.VMEM((LANES * PITCH, 2 * columns), jnp.float32),
            pltpu.VMEM((2 * columns * PITCH, LANES), jnp.float32),
            pltpu.VMEM((halves, channels, WIN_ROWS, samples), jnp.bfloat16),
            pltpu.VMEM((2, samples, 2 * columns), jnp.bfloat16),
            pltpu.SemaphoreType.DMA((halves, steps, 2)),
        ],
        compiler_params=pltpu.CompilerParams(vmem_limit_bytes=VMEM_BYTES),
        cost_estimate=pl.CostEstimate(flops=flops, bytes_accessed=traces.size * 2, transcendentals=0),
        name="spectra",
    )(lax.axis_index("win").reshape(1), traces)


def cut(found, low, high):
    cuts = {}
    for at, parts in found.items():
        cuts[at], start = [], 0
        for part in parts:
            first, last = max(low, start), min(high, start + part.shape[0])
            if first < last:
                cuts[at].append((part, first - start, last - first))
            start += part.shape[0]
    return cuts


def pick_kernel(places, far_ref, *refs):
    out_ref = refs[-1]
    for r in range(ROUNDS):
        for at in places:

            @pl.when(far_ref[r] == at)
            def _():
                row = 0
                for n, first, count in places[at]:
                    out_ref[r, row : row + count] = refs[n][first : first + count]
                    row += count


def pick(cuts, far):
    arrays, places = [], {at: [] for at in sorted(cuts[0])}
    for chunk in cuts:
        for at in places:
            for part, first, count in chunk[at]:
                places[at].append((len(arrays), first, count))
                arrays.append(part)
    rows = sum(count for _, _, count in places[0])
    whole = pl.BlockSpec(memory_space=pltpu.VMEM)
    return pl.pallas_call(
        functools.partial(pick_kernel, places),
        in_specs=[pl.BlockSpec(memory_space=pltpu.SMEM)] + [whole] * len(arrays),
        out_specs=whole,
        out_shape=jax.ShapeDtypeStruct((ROUNDS, rows, *arrays[0].shape[1:]), jnp.bfloat16),
        compiler_params=pltpu.CompilerParams(vmem_limit_bytes=VMEM_BYTES),
        name="pick",
    )(far, *arrays)


def left_kernel(*refs):
    own, out_ref = refs[:-1], refs[-1]
    channels = out_ref.shape[1] // 2

    @pl.loop(0, out_ref.shape[0])
    def _(bin_no):
        straight, turned = [], []
        for source in own:
            real, imag = source[2 * bin_no], source[2 * bin_no + 1]
            straight += [real, imag]
            turned += [imag, -real]
        out_ref[bin_no, :channels] = jnp.concatenate(straight, axis=0).T
        out_ref[bin_no, channels:] = jnp.concatenate(turned, axis=0).T


def left_side(own, windows):
    rows, _, channels = own[0].shape
    whole = pl.BlockSpec(memory_space=pltpu.VMEM)
    return pl.pallas_call(
        left_kernel,
        in_specs=[whole] * len(own),
        out_specs=whole,
        out_shape=jax.ShapeDtypeStruct((rows // 2, 2 * channels, 2 * windows), jnp.bfloat16),
        compiler_params=pltpu.CompilerParams(vmem_limit_bytes=VMEM_BYTES),
        name="left_side",
    )(*own)


def correlate_kernel(scale, layout, far_ref, left_ref, *refs):
    out_hbm, right_ref, result_ref, sems = refs[-4:]
    bins, _, _, channels, _ = result_ref.shape

    for r in range(ROUNDS):
        far = far_ref[r]

        @pl.when(far % 2 == 1)
        def _():
            for c, (across, _) in enumerate(layout):
                row = 0
                for n, first, count in across:
                    right_ref[r, c, row : row + count] = refs[n][r, first : first + count]
                    row += count

        for at in layout[0][1]:

            @pl.when(far == at)
            def _():
                for c, (_, by_key) in enumerate(layout):
                    row = 0
                    for n in by_key[at]:
                        count = refs[n].shape[0]
                        right_ref[r, c, row : row + count] = refs[n][...]
                        row += count

    def send(bin_no, r):
        return pltpu.make_async_copy(result_ref.at[bin_no, r], out_hbm.at[r, bin_no], sems.at[bin_no, r])

    @pl.loop(0, bins, unroll=2)
    def _(bin_no):
        for r in range(ROUNDS):
            right = jnp.concatenate(
                [right_ref[r, c, 2 * bin_no + part] for c in range(len(layout)) for part in range(2)], axis=0
            )
            product = jnp.dot(left_ref[bin_no], right, preferred_element_type=jnp.float32)
            result_ref[bin_no, r] = (product * scale).reshape(2, channels, channels)
            send(bin_no, r).start()

    @pl.loop(0, bins)
    def _(bin_no):
        for r in range(ROUNDS):
            send(bin_no, r).wait()


def correlate(far, left, found, across, other):
    bins, both, depth = left.shape
    channels = both // 2
    arrays, layout = list(across), []

    def numbered(parts):
        arrays.extend(parts)
        return list(range(len(arrays) - len(parts), len(arrays)))

    for chunk, parts in zip(found, other):
        layout.append((parts, {at: numbered(chunk[at]) for at in sorted(chunk) if at}))
    rows, windows_dev, _ = found[0][0][0].shape
    whole = pl.BlockSpec(memory_space=pltpu.VMEM)
    shape = (ROUNDS, bins, 2, channels, channels)
    flops = 4 * ROUNDS * bins * depth * channels * channels
    scale = 1.0 / math.sqrt(depth // 2)
    return pl.pallas_call(
        functools.partial(correlate_kernel, scale, layout),
        in_specs=[pl.BlockSpec(memory_space=pltpu.SMEM)] + [whole] * (1 + len(arrays)),
        out_specs=pl.BlockSpec(memory_space=pl.ANY),
        out_shape=jax.ShapeDtypeStruct(shape, jnp.float32),
        scratch_shapes=[
            pltpu.VMEM((ROUNDS, len(layout), rows, windows_dev, channels), jnp.bfloat16),
            pltpu.VMEM((bins, ROUNDS, 2, channels, channels), jnp.float32),
            pltpu.SemaphoreType.DMA((bins, ROUNDS)),
        ],
        compiler_params=pltpu.CompilerParams(vmem_limit_bytes=VMEM_BYTES),
        cost_estimate=pl.CostEstimate(flops=flops, bytes_accessed=4 * math.prod(shape), transcendentals=0),
        name="cross_spectra",
    )(far, left, *arrays)


def partner_positions(partner, block_ids, count):
    slots = jnp.arange(count, dtype=jnp.int32)
    holder = jnp.sum(jnp.where(block_ids[None, :] == slots[:, None], slots[None, :], 0), axis=1)
    at_block = block_ids[:, None] == slots[None, :]
    wanted = jnp.sum(jnp.where(at_block[None], partner[:, None, :], 0), axis=2)
    return jnp.sum(jnp.where(wanted[:, :, None] == slots, holder, 0), axis=2)


def swap(value, axis, distance):
    count = lax.axis_size(axis)
    return lax.ppermute(value, axis, [(i, i ^ distance) for i in range(count)])


def after(value, *others):
    return lax.optimization_barrier((value, *others))[0] if others else value


def gather_even(piece, relay):
    pair_count = lax.axis_size("pair")
    half = piece.shape[0] // 2
    found = {0: [piece]}
    for distance in range(2, pair_count, 2):
        if distance != 6 or not relay:
            found[distance] = [swap(piece, "pair", distance)]
    if relay and 6 < pair_count:
        found[6] = [swap(found[4][0][:half], "pair", 2), swap(found[2][0][half:], "pair", 4)]
    return found


def local(traces, partner, block_ids):
    pair_count = lax.axis_size("pair")
    win_count = lax.axis_size("win")
    rows = 2 * BINS // win_count
    windows = traces.shape[1] * win_count
    me = lax.axis_index("pair")
    slots = jnp.arange(pair_count, dtype=jnp.int32)
    paired = partner_positions(partner, block_ids, pair_count)
    mine = jnp.sum(jnp.where(slots == me, paired, 0), axis=1) ^ me
    beside = jnp.sum(jnp.where(slots == (me ^ 1), paired, 0), axis=1) ^ me

    sent = local_spectra(traces, win_count, [(s, 0, rows) for s in range(win_count)])
    own, found = [], []
    for s, piece in enumerate(sent):
        if s:
            piece = swap(after(piece, own[2]) if s == 3 else piece, "win", s)
        own.append(piece)
    for s, piece in enumerate(own):
        if s >= 1:
            near = [part for at in (2, 4) for part in found[s - 1].get(at, [])]
            piece = after(piece, *near, *(found[s - 2].get(6, []) if s == 2 else []))
        found.append(gather_even(piece, relay=s > 0))
    left = left_side(own, windows)
    half = rows // 2
    early = [swap(pick([cut(chunk, 0, rows)], beside), "pair", 1) for chunk in found[:-2]]
    late = [
        swap(pick([cut(chunk, at, at + half) for chunk in found[-2:]], beside), "pair", 1)
        for at in (0, half)
    ]
    other = [[(n, 0, rows)] for n in range(len(early))]
    for n in range(2):
        other.append([(len(early) + part, n * half, half) for part in range(2)])
    return correlate(mine, left, found, early + late, other)


def solution(mesh):
    placed = (P("pair", "win", None), P(), P())
    return jax.shard_map(
        local,
        mesh=mesh,
        in_specs=placed,
        out_specs=P(None, "win", None, "pair", None),
        check_vma=False,
    )
```

```python
import functools
import math

import jax
import jax.numpy as jnp
from jax import lax
from jax.experimental import pallas as pl
from jax.experimental.pallas import tpu as pltpu
from jax.sharding import PartitionSpec as P

BINS = 32
FIRST_BIN = 16
BIN_STEP = 8
ROUNDS = 2
LANES = 128
WIN_ROWS = 16
PITCH = 20
VMEM_BYTES = 44 * 1024 * 1024


def fill_table(table_ref):
    samples, columns = table_ref.shape[1], 2 * BINS
    period = samples // math.gcd(FIRST_BIN, BIN_STEP, samples)
    step = 2.0 * math.pi / samples
    sample = lax.broadcasted_iota(jnp.int32, (period, LANES), 0)
    column = lax.broadcasted_iota(jnp.int32, (period, LANES), 1) & (columns - 1)
    freq = FIRST_BIN + BIN_STEP * (column >> 1)
    angle = step * ((sample * freq) & (samples - 1)).astype(jnp.float32)
    waves = jnp.where((column & 1) == 0, jnp.cos(angle), -jnp.sin(angle))
    around = step * sample.astype(jnp.float32)
    cosine, sine = jnp.cos(around), jnp.sin(around)
    low = lax.broadcasted_iota(jnp.int32, (period, LANES), 1) < columns
    for n in range(samples // period):
        turn = 2.0 * math.pi * n * period / samples
        taper = 0.5 - 0.5 * (math.cos(turn) * cosine - math.sin(turn) * sine)
        tapered = taper * waves
        rows = slice(n * period, (n + 1) * period)
        table_ref[0, rows] = jnp.where(low, tapered, 0.0).astype(jnp.bfloat16)
        table_ref[1, rows] = jnp.where(low, 0.0, tapered).astype(jnp.bfloat16)


def spectra_kernel(chan_rows, win_count, pieces, win_ref, traces_ref, *rest):
    outs = rest[: len(pieces)]
    raw_ref, turned_ref, traces_buf, table_ref, sems = rest[len(pieces) :]
    columns = 2 * BINS
    per = columns // win_count
    samples = traces_ref.shape[2]
    steps = LANES // chan_rows
    halves = traces_ref.shape[1] // WIN_ROWS
    rows = chan_rows * WIN_ROWS

    def copy(h, i, g):
        first = g * LANES + i * chan_rows
        return pltpu.make_async_copy(
            traces_ref.at[pl.ds(first, chan_rows), pl.ds(h * WIN_ROWS, WIN_ROWS), :],
            traces_buf.at[h, pl.ds(first, chan_rows)],
            sems.at[h, i, g],
        )

    for h in range(halves):

        @pl.loop(0, steps)
        def _(i):
            copy(h, i, 0).start()
            copy(h, i, 1).start()

    fill_table(table_ref)
    for h in range(halves):

        @pl.loop(0, steps)
        def _(i):
            copy(h, i, 0).wait()
            copy(h, i, 1).wait()
            low = traces_buf[h, pl.ds(i * chan_rows, chan_rows)].reshape(rows, samples)
            high = traces_buf[h, pl.ds(LANES + i * chan_rows, chan_rows)].reshape(rows, samples)
            raw = jnp.dot(low, table_ref[0], preferred_element_type=jnp.float32)
            raw += jnp.dot(high, table_ref[1], preferred_element_type=jnp.float32)
            base = pl.multiple_of(i * (chan_rows * PITCH), 8)
            for c in range(chan_rows):
                raw_ref[pl.ds(base + c * PITCH, WIN_ROWS), :] = raw[c * WIN_ROWS : (c + 1) * WIN_ROWS]

        for w in range(WIN_ROWS):
            turned = raw_ref[pl.ds(w, LANES, stride=PITCH), :].T
            for g in range(2):
                part = turned[g * columns : (g + 1) * columns]
                power = jnp.mean(part * part, axis=0, keepdims=True)
                first = g * columns * PITCH + w
                turned_ref[pl.ds(first, columns, stride=PITCH), :] = part * lax.rsqrt(power + 1e-05)
        for out_ref, (s, low, high) in zip(outs, pieces):
            base = pl.multiple_of((win_ref[0] ^ s) * (per * PITCH), 8)
            for g in range(2):
                for k in range(low, high):
                    taken = turned_ref[pl.ds(base + (g * columns + k) * PITCH, WIN_ROWS), :]
                    out_ref[k - low, h * WIN_ROWS : (h + 1) * WIN_ROWS, g * LANES : (g + 1) * LANES] = (
                        taken.astype(jnp.bfloat16)
                    )


def local_spectra(traces, win_count, pieces):
    channels, windows, samples = traces.shape
    columns = 2 * BINS
    chan_rows = 32
    steps, halves = LANES // chan_rows, windows // WIN_ROWS
    flops = 2 * channels * windows * samples * columns
    return pl.pallas_call(
        functools.partial(spectra_kernel, chan_rows, win_count, pieces),
        in_specs=[
            pl.BlockSpec(memory_space=pltpu.SMEM),
            pl.BlockSpec(memory_space=pl.ANY),
        ],
        out_specs=[pl.BlockSpec(memory_space=pltpu.VMEM)] * len(pieces),
        out_shape=[
            jax.ShapeDtypeStruct((high - low, windows, channels), jnp.bfloat16) for _, low, high in pieces
        ],
        scratch_shapes=[
            pltpu.VMEM((LANES * PITCH, 2 * columns), jnp.float32),
            pltpu.VMEM((2 * columns * PITCH, LANES), jnp.float32),
            pltpu.VMEM((halves, channels, WIN_ROWS, samples), jnp.bfloat16),
            pltpu.VMEM((2, samples, 2 * columns), jnp.bfloat16),
            pltpu.SemaphoreType.DMA((halves, steps, 2)),
        ],
        compiler_params=pltpu.CompilerParams(vmem_limit_bytes=VMEM_BYTES),
        cost_estimate=pl.CostEstimate(flops=flops, bytes_accessed=traces.size * 2, transcendentals=0),
        name="spectra",
    )(lax.axis_index("win").reshape(1), traces)


def cut(found, low, high):
    cuts = {}
    for at, parts in found.items():
        cuts[at], start = [], 0
        for part in parts:
            first, last = max(low, start), min(high, start + part.shape[0])
            if first < last:
                cuts[at].append((part, first - start, last - first))
            start += part.shape[0]
    return cuts


def pick_kernel(places, far_ref, *refs):
    out_ref = refs[-1]
    for r in range(ROUNDS):
        for at in places:

            @pl.when(far_ref[r] == at)
            def _():
                row = 0
                for n, first, count in places[at]:
                    out_ref[r, row : row + count] = refs[n][first : first + count]
                    row += count


def pick(cuts, far):
    arrays, places = [], {at: [] for at in sorted(cuts[0])}
    for chunk in cuts:
        for at in places:
            for part, first, count in chunk[at]:
                places[at].append((len(arrays), first, count))
                arrays.append(part)
    rows = sum(count for _, _, count in places[0])
    whole = pl.BlockSpec(memory_space=pltpu.VMEM)
    return pl.pallas_call(
        functools.partial(pick_kernel, places),
        in_specs=[pl.BlockSpec(memory_space=pltpu.SMEM)] + [whole] * len(arrays),
        out_specs=whole,
        out_shape=jax.ShapeDtypeStruct((ROUNDS, rows, *arrays[0].shape[1:]), jnp.bfloat16),
        compiler_params=pltpu.CompilerParams(vmem_limit_bytes=VMEM_BYTES),
        name="pick",
    )(far, *arrays)


def left_kernel(*refs):
    own, out_ref = refs[:-1], refs[-1]
    channels = out_ref.shape[1] // 2

    @pl.loop(0, out_ref.shape[0])
    def _(bin_no):
        straight, turned = [], []
        for source in own:
            real, imag = source[2 * bin_no], source[2 * bin_no + 1]
            straight += [real, imag]
            turned += [imag, -real]
        out_ref[bin_no, :channels] = jnp.concatenate(straight, axis=0).T
        out_ref[bin_no, channels:] = jnp.concatenate(turned, axis=0).T


def left_side(own, windows):
    rows, _, channels = own[0].shape
    whole = pl.BlockSpec(memory_space=pltpu.VMEM)
    return pl.pallas_call(
        left_kernel,
        in_specs=[whole] * len(own),
        out_specs=whole,
        out_shape=jax.ShapeDtypeStruct((rows // 2, 2 * channels, 2 * windows), jnp.bfloat16),
        compiler_params=pltpu.CompilerParams(vmem_limit_bytes=VMEM_BYTES),
        name="left_side",
    )(*own)


def correlate_kernel(scale, layout, far_ref, left_ref, *refs):
    out_hbm, right_ref, result_ref, sems = refs[-4:]
    bins, _, _, channels, _ = result_ref.shape

    for r in range(ROUNDS):
        far = far_ref[r]

        @pl.when(far % 2 == 1)
        def _():
            for c, (across, _) in enumerate(layout):
                row = 0
                for n, first, count in across:
                    right_ref[r, c, row : row + count] = refs[n][r, first : first + count]
                    row += count

        for at in layout[0][1]:

            @pl.when(far == at)
            def _():
                for c, (_, by_key) in enumerate(layout):
                    row = 0
                    for n in by_key[at]:
                        count = refs[n].shape[0]
                        right_ref[r, c, row : row + count] = refs[n][...]
                        row += count

    def send(bin_no, r):
        return pltpu.make_async_copy(result_ref.at[bin_no, r], out_hbm.at[r, bin_no], sems.at[bin_no, r])

    @pl.loop(0, bins, unroll=2)
    def _(bin_no):
        for r in range(ROUNDS):
            right = jnp.concatenate(
                [right_ref[r, c, 2 * bin_no + part] for c in range(len(layout)) for part in range(2)], axis=0
            )
            product = jnp.dot(left_ref[bin_no], right, preferred_element_type=jnp.float32)
            result_ref[bin_no, r] = (product * scale).reshape(2, channels, channels)
            send(bin_no, r).start()

    @pl.loop(0, bins)
    def _(bin_no):
        for r in range(ROUNDS):
            send(bin_no, r).wait()


def correlate(far, left, found, across, other):
    bins, both, depth = left.shape
    channels = both // 2
    arrays, layout = list(across), []

    def numbered(parts):
        arrays.extend(parts)
        return list(range(len(arrays) - len(parts), len(arrays)))

    for chunk, parts in zip(found, other):
        layout.append((parts, {at: numbered(chunk[at]) for at in sorted(chunk) if at}))
    rows, windows_dev, _ = found[0][0][0].shape
    whole = pl.BlockSpec(memory_space=pltpu.VMEM)
    shape = (ROUNDS, bins, 2, channels, channels)
    flops = 4 * ROUNDS * bins * depth * channels * channels
    scale = 1.0 / math.sqrt(depth // 2)
    return pl.pallas_call(
        functools.partial(correlate_kernel, scale, layout),
        in_specs=[pl.BlockSpec(memory_space=pltpu.SMEM)] + [whole] * (1 + len(arrays)),
        out_specs=pl.BlockSpec(memory_space=pl.ANY),
        out_shape=jax.ShapeDtypeStruct(shape, jnp.float32),
        scratch_shapes=[
            pltpu.VMEM((ROUNDS, len(layout), rows, windows_dev, channels), jnp.bfloat16),
            pltpu.VMEM((bins, ROUNDS, 2, channels, channels), jnp.float32),
            pltpu.SemaphoreType.DMA((bins, ROUNDS)),
        ],
        compiler_params=pltpu.CompilerParams(vmem_limit_bytes=VMEM_BYTES),
        cost_estimate=pl.CostEstimate(flops=flops, bytes_accessed=4 * math.prod(shape), transcendentals=0),
        name="cross_spectra",
    )(far, left, *arrays)


def partner_positions(partner, block_ids, count):
    slots = jnp.arange(count, dtype=jnp.int32)
    holder = jnp.sum(jnp.where(block_ids[None, :] == slots[:, None], slots[None, :], 0), axis=1)
    at_block = block_ids[:, None] == slots[None, :]
    wanted = jnp.sum(jnp.where(at_block[None], partner[:, None, :], 0), axis=2)
    return jnp.sum(jnp.where(wanted[:, :, None] == slots, holder, 0), axis=2)


def swap(value, axis, distance):
    count = lax.axis_size(axis)
    return lax.ppermute(value, axis, [(i, i ^ distance) for i in range(count)])


def after(value, *others):
    return lax.optimization_barrier((value, *others))[0] if others else value


def gather_even(piece, relay):
    pair_count = lax.axis_size("pair")
    half = piece.shape[0] // 2
    found = {0: [piece]}
    for distance in range(2, pair_count, 2):
        if distance != 6 or not relay:
            found[distance] = [swap(piece, "pair", distance)]
    if relay and 6 < pair_count:
        found[6] = [swap(found[4][0][:half], "pair", 2), swap(found[2][0][half:], "pair", 4)]
    return found


def local(traces, partner, block_ids):
    pair_count = lax.axis_size("pair")
    win_count = lax.axis_size("win")
    rows = 2 * BINS // win_count
    windows = traces.shape[1] * win_count
    me = lax.axis_index("pair")
    slots = jnp.arange(pair_count, dtype=jnp.int32)
    paired = partner_positions(partner, block_ids, pair_count)
    mine = jnp.sum(jnp.where(slots == me, paired, 0), axis=1) ^ me
    beside = jnp.sum(jnp.where(slots == (me ^ 1), paired, 0), axis=1) ^ me

    sent = local_spectra(traces, win_count, [(s, 0, rows) for s in range(win_count)])
    own, found = [], []
    for s, piece in enumerate(sent):
        if s:
            piece = swap(after(piece, own[2], own[1]) if s == 3 else piece, "win", s)
        own.append(piece)
    for s, piece in enumerate(own):
        if s >= 1:
            near = [part for at in (2, 4) for part in found[s - 1].get(at, [])]
            piece = after(piece, *(near if s < 3 else near[:1]), *(found[s - 2].get(6, []) if s == 2 else []))
        found.append(gather_even(piece, relay=s > 0))
    left = left_side(own, windows)
    half = rows // 2
    early = [swap(pick([cut(chunk, 0, rows)], beside), "pair", 1) for chunk in found[:-2]]
    late = [
        swap(pick([cut(chunk, at, at + half) for chunk in found[-2:]], beside), "pair", 1)
        for at in (0, half)
    ]
    other = [[(n, 0, rows)] for n in range(len(early))]
    for n in range(2):
        other.append([(len(early) + part, n * half, half) for part in range(2)])
    return correlate(mine, left, found, early + late, other)


def solution(mesh):
    placed = (P("pair", "win", None), P(), P())
    return jax.shard_map(
        local,
        mesh=mesh,
        in_specs=placed,
        out_specs=P(None, "win", None, "pair", None),
        check_vma=False,
    )
```

```python
import functools
import math

import jax
import jax.numpy as jnp
from jax import lax
from jax.experimental import pallas as pl
from jax.experimental.pallas import tpu as pltpu
from jax.sharding import PartitionSpec as P

BINS = 32
FIRST_BIN = 16
BIN_STEP = 8
ROUNDS = 2
LANES = 128
WIN_ROWS = 16
PITCH = 20
VMEM_BYTES = 44 * 1024 * 1024


def fill_table(table_ref):
    samples, columns = table_ref.shape[1], 2 * BINS
    period = samples // math.gcd(FIRST_BIN, BIN_STEP, samples)
    step = 2.0 * math.pi / samples
    sample = lax.broadcasted_iota(jnp.int32, (period, LANES), 0)
    column = lax.broadcasted_iota(jnp.int32, (period, LANES), 1) & (columns - 1)
    freq = FIRST_BIN + BIN_STEP * (column >> 1)
    angle = step * ((sample * freq) & (samples - 1)).astype(jnp.float32)
    waves = jnp.where((column & 1) == 0, jnp.cos(angle), -jnp.sin(angle))
    around = step * sample.astype(jnp.float32)
    cosine, sine = jnp.cos(around), jnp.sin(around)
    low = lax.broadcasted_iota(jnp.int32, (period, LANES), 1) < columns
    for n in range(samples // period):
        turn = 2.0 * math.pi * n * period / samples
        taper = 0.5 - 0.5 * (math.cos(turn) * cosine - math.sin(turn) * sine)
        tapered = taper * waves
        rows = slice(n * period, (n + 1) * period)
        table_ref[0, rows] = jnp.where(low, tapered, 0.0).astype(jnp.bfloat16)
        table_ref[1, rows] = jnp.where(low, 0.0, tapered).astype(jnp.bfloat16)


def spectra_kernel(chan_rows, win_count, pieces, win_ref, traces_ref, *rest):
    outs = rest[: len(pieces)]
    raw_ref, turned_ref, traces_buf, table_ref, sems = rest[len(pieces) :]
    columns = 2 * BINS
    per = columns // win_count
    samples = traces_ref.shape[2]
    steps = LANES // chan_rows
    halves = traces_ref.shape[1] // WIN_ROWS
    rows = chan_rows * WIN_ROWS

    def copy(h, i, g):
        first = g * LANES + i * chan_rows
        return pltpu.make_async_copy(
            traces_ref.at[pl.ds(first, chan_rows), pl.ds(h * WIN_ROWS, WIN_ROWS), :],
            traces_buf.at[h, pl.ds(first, chan_rows)],
            sems.at[h, i, g],
        )

    for h in range(halves):

        @pl.loop(0, steps)
        def _(i):
            copy(h, i, 0).start()
            copy(h, i, 1).start()

    fill_table(table_ref)
    for h in range(halves):

        @pl.loop(0, steps)
        def _(i):
            copy(h, i, 0).wait()
            copy(h, i, 1).wait()
            low = traces_buf[h, pl.ds(i * chan_rows, chan_rows)].reshape(rows, samples)
            high = traces_buf[h, pl.ds(LANES + i * chan_rows, chan_rows)].reshape(rows, samples)
            raw = jnp.dot(low, table_ref[0], preferred_element_type=jnp.float32)
            raw += jnp.dot(high, table_ref[1], preferred_element_type=jnp.float32)
            base = pl.multiple_of(i * (chan_rows * PITCH), 8)
            for c in range(chan_rows):
                raw_ref[pl.ds(base + c * PITCH, WIN_ROWS), :] = raw[c * WIN_ROWS : (c + 1) * WIN_ROWS]

        for w in range(WIN_ROWS):
            turned = raw_ref[pl.ds(w, LANES, stride=PITCH), :].T
            for g in range(2):
                part = turned[g * columns : (g + 1) * columns]
                power = jnp.mean(part * part, axis=0, keepdims=True)
                first = g * columns * PITCH + w
                turned_ref[pl.ds(first, columns, stride=PITCH), :] = part * lax.rsqrt(power + 1e-05)
        for out_ref, (s, low, high) in zip(outs, pieces):
            base = pl.multiple_of((win_ref[0] ^ s) * (per * PITCH), 8)
            for g in range(2):
                for k in range(low, high):
                    taken = turned_ref[pl.ds(base + (g * columns + k) * PITCH, WIN_ROWS), :]
                    out_ref[k - low, h * WIN_ROWS : (h + 1) * WIN_ROWS, g * LANES : (g + 1) * LANES] = (
                        taken.astype(jnp.bfloat16)
                    )


def local_spectra(traces, win_count, pieces):
    channels, windows, samples = traces.shape
    columns = 2 * BINS
    chan_rows = 64
    steps, halves = LANES // chan_rows, windows // WIN_ROWS
    flops = 2 * channels * windows * samples * columns
    return pl.pallas_call(
        functools.partial(spectra_kernel, chan_rows, win_count, pieces),
        in_specs=[
            pl.BlockSpec(memory_space=pltpu.SMEM),
            pl.BlockSpec(memory_space=pl.ANY),
        ],
        out_specs=[pl.BlockSpec(memory_space=pltpu.VMEM)] * len(pieces),
        out_shape=[
            jax.ShapeDtypeStruct((high - low, windows, channels), jnp.bfloat16) for _, low, high in pieces
        ],
        scratch_shapes=[
            pltpu.VMEM((LANES * PITCH, 2 * columns), jnp.float32),
            pltpu.VMEM((2 * columns * PITCH, LANES), jnp.float32),
            pltpu.VMEM((halves, channels, WIN_ROWS, samples), jnp.bfloat16),
            pltpu.VMEM((2, samples, 2 * columns), jnp.bfloat16),
            pltpu.SemaphoreType.DMA((halves, steps, 2)),
        ],
        compiler_params=pltpu.CompilerParams(vmem_limit_bytes=VMEM_BYTES),
        cost_estimate=pl.CostEstimate(flops=flops, bytes_accessed=traces.size * 2, transcendentals=0),
        name="spectra",
    )(lax.axis_index("win").reshape(1), traces)


def cut(found, low, high):
    cuts = {}
    for at, parts in found.items():
        cuts[at], start = [], 0
        for part in parts:
            first, last = max(low, start), min(high, start + part.shape[0])
            if first < last:
                cuts[at].append((part, first - start, last - first))
            start += part.shape[0]
    return cuts


def pick_kernel(places, far_ref, *refs):
    out_ref = refs[-1]
    for r in range(ROUNDS):
        for at in places:

            @pl.when(far_ref[r] == at)
            def _():
                row = 0
                for n, first, count in places[at]:
                    out_ref[r, row : row + count] = refs[n][first : first + count]
                    row += count


def pick(cuts, far):
    arrays, places = [], {at: [] for at in sorted(cuts[0])}
    for chunk in cuts:
        for at in places:
            for part, first, count in chunk[at]:
                places[at].append((len(arrays), first, count))
                arrays.append(part)
    rows = sum(count for _, _, count in places[0])
    whole = pl.BlockSpec(memory_space=pltpu.VMEM)
    return pl.pallas_call(
        functools.partial(pick_kernel, places),
        in_specs=[pl.BlockSpec(memory_space=pltpu.SMEM)] + [whole] * len(arrays),
        out_specs=whole,
        out_shape=jax.ShapeDtypeStruct((ROUNDS, rows, *arrays[0].shape[1:]), jnp.bfloat16),
        compiler_params=pltpu.CompilerParams(vmem_limit_bytes=VMEM_BYTES),
        name="pick",
    )(far, *arrays)


def left_kernel(*refs):
    own, out_ref = refs[:-1], refs[-1]
    channels = out_ref.shape[1] // 2

    @pl.loop(0, out_ref.shape[0])
    def _(bin_no):
        straight, turned = [], []
        for source in own:
            real, imag = source[2 * bin_no], source[2 * bin_no + 1]
            straight += [real, imag]
            turned += [imag, -real]
        out_ref[bin_no, :channels] = jnp.concatenate(straight, axis=0).T
        out_ref[bin_no, channels:] = jnp.concatenate(turned, axis=0).T


def left_side(own, windows):
    rows, _, channels = own[0].shape
    whole = pl.BlockSpec(memory_space=pltpu.VMEM)
    return pl.pallas_call(
        left_kernel,
        in_specs=[whole] * len(own),
        out_specs=whole,
        out_shape=jax.ShapeDtypeStruct((rows // 2, 2 * channels, 2 * windows), jnp.bfloat16),
        compiler_params=pltpu.CompilerParams(vmem_limit_bytes=VMEM_BYTES),
        name="left_side",
    )(*own)


def correlate_kernel(scale, layout, far_ref, left_ref, *refs):
    out_hbm, right_ref, result_ref, sems = refs[-4:]
    bins, _, _, channels, _ = result_ref.shape

    for r in range(ROUNDS):
        far = far_ref[r]

        @pl.when(far % 2 == 1)
        def _():
            for c, (across, _) in enumerate(layout):
                row = 0
                for n, first, count in across:
                    right_ref[r, c, row : row + count] = refs[n][r, first : first + count]
                    row += count

        for at in layout[0][1]:

            @pl.when(far == at)
            def _():
                for c, (_, by_key) in enumerate(layout):
                    row = 0
                    for n in by_key[at]:
                        count = refs[n].shape[0]
                        right_ref[r, c, row : row + count] = refs[n][...]
                        row += count

    def send(bin_no, r):
        return pltpu.make_async_copy(result_ref.at[bin_no, r], out_hbm.at[r, bin_no], sems.at[bin_no, r])

    @pl.loop(0, bins, unroll=2)
    def _(bin_no):
        for r in range(ROUNDS):
            right = jnp.concatenate(
                [right_ref[r, c, 2 * bin_no + part] for c in range(len(layout)) for part in range(2)], axis=0
            )
            product = jnp.dot(left_ref[bin_no], right, preferred_element_type=jnp.float32)
            result_ref[bin_no, r] = (product * scale).reshape(2, channels, channels)
            send(bin_no, r).start()

    @pl.loop(0, bins)
    def _(bin_no):
        for r in range(ROUNDS):
            send(bin_no, r).wait()


def correlate(far, left, found, across, other):
    bins, both, depth = left.shape
    channels = both // 2
    arrays, layout = list(across), []

    def numbered(parts):
        arrays.extend(parts)
        return list(range(len(arrays) - len(parts), len(arrays)))

    for chunk, parts in zip(found, other):
        layout.append((parts, {at: numbered(chunk[at]) for at in sorted(chunk) if at}))
    rows, windows_dev, _ = found[0][0][0].shape
    whole = pl.BlockSpec(memory_space=pltpu.VMEM)
    shape = (ROUNDS, bins, 2, channels, channels)
    flops = 4 * ROUNDS * bins * depth * channels * channels
    scale = 1.0 / math.sqrt(depth // 2)
    return pl.pallas_call(
        functools.partial(correlate_kernel, scale, layout),
        in_specs=[pl.BlockSpec(memory_space=pltpu.SMEM)] + [whole] * (1 + len(arrays)),
        out_specs=pl.BlockSpec(memory_space=pl.ANY),
        out_shape=jax.ShapeDtypeStruct(shape, jnp.float32),
        scratch_shapes=[
            pltpu.VMEM((ROUNDS, len(layout), rows, windows_dev, channels), jnp.bfloat16),
            pltpu.VMEM((bins, ROUNDS, 2, channels, channels), jnp.float32),
            pltpu.SemaphoreType.DMA((bins, ROUNDS)),
        ],
        compiler_params=pltpu.CompilerParams(vmem_limit_bytes=VMEM_BYTES),
        cost_estimate=pl.CostEstimate(flops=flops, bytes_accessed=4 * math.prod(shape), transcendentals=0),
        name="cross_spectra",
    )(far, left, *arrays)


def partner_positions(partner, block_ids, count):
    slots = jnp.arange(count, dtype=jnp.int32)
    holder = jnp.sum(jnp.where(block_ids[None, :] == slots[:, None], slots[None, :], 0), axis=1)
    at_block = block_ids[:, None] == slots[None, :]
    wanted = jnp.sum(jnp.where(at_block[None], partner[:, None, :], 0), axis=2)
    return jnp.sum(jnp.where(wanted[:, :, None] == slots, holder, 0), axis=2)


def swap(value, axis, distance):
    count = lax.axis_size(axis)
    return lax.ppermute(value, axis, [(i, i ^ distance) for i in range(count)])


def after(value, *others):
    return lax.optimization_barrier((value, *others))[0] if others else value


def gather_even(piece, relay):
    pair_count = lax.axis_size("pair")
    half = piece.shape[0] // 2
    found = {0: [piece]}
    for distance in range(2, pair_count, 2):
        if distance != 6 or not relay:
            found[distance] = [swap(piece, "pair", distance)]
    if relay and 6 < pair_count:
        found[6] = [swap(found[4][0][:half], "pair", 2), swap(found[2][0][half:], "pair", 4)]
    return found


def local(traces, partner, block_ids):
    pair_count = lax.axis_size("pair")
    win_count = lax.axis_size("win")
    rows = 2 * BINS // win_count
    windows = traces.shape[1] * win_count
    me = lax.axis_index("pair")
    slots = jnp.arange(pair_count, dtype=jnp.int32)
    paired = partner_positions(partner, block_ids, pair_count)
    mine = jnp.sum(jnp.where(slots == me, paired, 0), axis=1) ^ me
    beside = jnp.sum(jnp.where(slots == (me ^ 1), paired, 0), axis=1) ^ me

    sent = local_spectra(traces, win_count, [(s, 0, rows) for s in range(win_count)])
    own, found = [], []
    for s, piece in enumerate(sent):
        if s:
            piece = swap(after(piece, own[2], own[1]) if s == 3 else piece, "win", s)
        own.append(piece)
    for s, piece in enumerate(own):
        if s >= 1:
            near = [part for at in (2, 4) for part in found[s - 1].get(at, [])]
            piece = after(piece, *(near if s < 3 else near[:1]), *(found[s - 2].get(6, []) if s == 2 else []))
        found.append(gather_even(piece, relay=s > 0))
    left = left_side(own, windows)
    half = rows // 2
    early = [swap(pick([cut(chunk, 0, rows)], beside), "pair", 1) for chunk in found[:-2]]
    late = [
        swap(pick([cut(chunk, at, at + half) for chunk in found[-2:]], beside), "pair", 1)
        for at in (0, half)
    ]
    other = [[(n, 0, rows)] for n in range(len(early))]
    for n in range(2):
        other.append([(len(early) + part, n * half, half) for part in range(2)])
    return correlate(mine, left, found, early + late, other)


def solution(mesh):
    placed = (P("pair", "win", None), P(), P())
    return jax.shard_map(
        local,
        mesh=mesh,
        in_specs=placed,
        out_specs=P(None, "win", None, "pair", None),
        check_vma=False,
    )
```

```python
import functools
import math

import jax
import jax.numpy as jnp
from jax import lax
from jax.experimental import pallas as pl
from jax.experimental.pallas import tpu as pltpu
from jax.sharding import PartitionSpec as P

BINS = 32
FIRST_BIN = 16
BIN_STEP = 8
ROUNDS = 2
LANES = 128
WIN_ROWS = 16
PITCH = 20
VMEM_BYTES = 44 * 1024 * 1024


def fill_table(table_ref):
    samples, columns = table_ref.shape[1], 2 * BINS
    period = samples // math.gcd(FIRST_BIN, BIN_STEP, samples)
    step = 2.0 * math.pi / samples
    sample = lax.broadcasted_iota(jnp.int32, (period, LANES), 0)
    column = lax.broadcasted_iota(jnp.int32, (period, LANES), 1) & (columns - 1)
    freq = FIRST_BIN + BIN_STEP * (column >> 1)
    angle = step * ((sample * freq) & (samples - 1)).astype(jnp.float32)
    waves = jnp.where((column & 1) == 0, jnp.cos(angle), -jnp.sin(angle))
    around = step * sample.astype(jnp.float32)
    cosine, sine = jnp.cos(around), jnp.sin(around)
    low = lax.broadcasted_iota(jnp.int32, (period, LANES), 1) < columns
    for n in range(samples // period):
        turn = 2.0 * math.pi * n * period / samples
        taper = 0.5 - 0.5 * (math.cos(turn) * cosine - math.sin(turn) * sine)
        tapered = taper * waves
        rows = slice(n * period, (n + 1) * period)
        table_ref[0, rows] = jnp.where(low, tapered, 0.0).astype(jnp.bfloat16)
        table_ref[1, rows] = jnp.where(low, 0.0, tapered).astype(jnp.bfloat16)


def spectra_kernel(chan_rows, win_count, pieces, win_ref, traces_ref, *rest):
    outs = rest[: len(pieces)]
    raw_ref, turned_ref, traces_buf, table_ref, sems = rest[len(pieces) :]
    columns = 2 * BINS
    per = columns // win_count
    samples = traces_ref.shape[2]
    steps = LANES // chan_rows
    halves = traces_ref.shape[1] // WIN_ROWS
    rows = chan_rows * WIN_ROWS

    def copy(h, i, g):
        first = g * LANES + i * chan_rows
        return pltpu.make_async_copy(
            traces_ref.at[pl.ds(first, chan_rows), pl.ds(h * WIN_ROWS, WIN_ROWS), :],
            traces_buf.at[h, pl.ds(first, chan_rows)],
            sems.at[h, i, g],
        )

    for h in range(halves):

        @pl.loop(0, steps)
        def _(i):
            copy(h, i, 0).start()
            copy(h, i, 1).start()

    fill_table(table_ref)
    for h in range(halves):

        @pl.loop(0, steps)
        def _(i):
            copy(h, i, 0).wait()
            copy(h, i, 1).wait()
            low = traces_buf[h, pl.ds(i * chan_rows, chan_rows)].reshape(rows, samples)
            high = traces_buf[h, pl.ds(LANES + i * chan_rows, chan_rows)].reshape(rows, samples)
            raw = jnp.dot(low, table_ref[0], preferred_element_type=jnp.float32)
            raw += jnp.dot(high, table_ref[1], preferred_element_type=jnp.float32)
            base = pl.multiple_of(i * (chan_rows * PITCH), 8)
            for c in range(chan_rows):
                raw_ref[pl.ds(base + c * PITCH, WIN_ROWS), :] = raw[c * WIN_ROWS : (c + 1) * WIN_ROWS]

        for w in range(WIN_ROWS):
            turned = raw_ref[pl.ds(w, LANES, stride=PITCH), :].T
            for g in range(2):
                part = turned[g * columns : (g + 1) * columns]
                power = jnp.mean(part * part, axis=0, keepdims=True)
                first = g * columns * PITCH + w
                turned_ref[pl.ds(first, columns, stride=PITCH), :] = part * lax.rsqrt(power + 1e-05)
        for out_ref, (s, low, high) in zip(outs, pieces):
            base = pl.multiple_of((win_ref[0] ^ s) * (per * PITCH), 8)
            for g in range(2):
                for k in range(low, high):
                    taken = turned_ref[pl.ds(base + (g * columns + k) * PITCH, WIN_ROWS), :]
                    out_ref[k - low, h * WIN_ROWS : (h + 1) * WIN_ROWS, g * LANES : (g + 1) * LANES] = (
                        taken.astype(jnp.bfloat16)
                    )


def local_spectra(traces, win_count, pieces):
    channels, windows, samples = traces.shape
    columns = 2 * BINS
    chan_rows = 64
    steps, halves = LANES // chan_rows, windows // WIN_ROWS
    flops = 2 * channels * windows * samples * columns
    return pl.pallas_call(
        functools.partial(spectra_kernel, chan_rows, win_count, pieces),
        in_specs=[
            pl.BlockSpec(memory_space=pltpu.SMEM),
            pl.BlockSpec(memory_space=pl.ANY),
        ],
        out_specs=[pl.BlockSpec(memory_space=pltpu.VMEM)] * len(pieces),
        out_shape=[
            jax.ShapeDtypeStruct((high - low, windows, channels), jnp.bfloat16) for _, low, high in pieces
        ],
        scratch_shapes=[
            pltpu.VMEM((LANES * PITCH, 2 * columns), jnp.float32),
            pltpu.VMEM((2 * columns * PITCH, LANES), jnp.float32),
            pltpu.VMEM((halves, channels, WIN_ROWS, samples), jnp.bfloat16),
            pltpu.VMEM((2, samples, 2 * columns), jnp.bfloat16),
            pltpu.SemaphoreType.DMA((halves, steps, 2)),
        ],
        compiler_params=pltpu.CompilerParams(vmem_limit_bytes=VMEM_BYTES),
        cost_estimate=pl.CostEstimate(flops=flops, bytes_accessed=traces.size * 2, transcendentals=0),
        name="spectra",
    )(lax.axis_index("win").reshape(1), traces)


def cut(found, low, high):
    cuts = {}
    for at, parts in found.items():
        cuts[at], start = [], 0
        for part in parts:
            first, last = max(low, start), min(high, start + part.shape[0])
            if first < last:
                cuts[at].append((part, first - start, last - first))
            start += part.shape[0]
    return cuts


def pick_kernel(places, far_ref, *refs):
    out_ref = refs[-1]
    for r in range(ROUNDS):
        for at in places:

            @pl.when(far_ref[r] == at)
            def _():
                row = 0
                for n, first, count in places[at]:
                    out_ref[r, row : row + count] = refs[n][first : first + count]
                    row += count


def pick(cuts, far):
    arrays, places = [], {at: [] for at in sorted(cuts[0])}
    for chunk in cuts:
        for at in places:
            for part, first, count in chunk[at]:
                places[at].append((len(arrays), first, count))
                arrays.append(part)
    rows = sum(count for _, _, count in places[0])
    whole = pl.BlockSpec(memory_space=pltpu.VMEM)
    return pl.pallas_call(
        functools.partial(pick_kernel, places),
        in_specs=[pl.BlockSpec(memory_space=pltpu.SMEM)] + [whole] * len(arrays),
        out_specs=whole,
        out_shape=jax.ShapeDtypeStruct((ROUNDS, rows, *arrays[0].shape[1:]), jnp.bfloat16),
        compiler_params=pltpu.CompilerParams(vmem_limit_bytes=VMEM_BYTES),
        name="pick",
    )(far, *arrays)


def left_kernel(*refs):
    own, out_ref = refs[:-1], refs[-1]
    channels = out_ref.shape[1] // 2

    @pl.loop(0, out_ref.shape[0])
    def _(bin_no):
        straight, turned = [], []
        for source in own:
            real, imag = source[2 * bin_no], source[2 * bin_no + 1]
            straight += [real, imag]
            turned += [imag, -real]
        out_ref[bin_no, :channels] = jnp.concatenate(straight, axis=0).T
        out_ref[bin_no, channels:] = jnp.concatenate(turned, axis=0).T


def left_side(own, windows):
    rows, _, channels = own[0].shape
    whole = pl.BlockSpec(memory_space=pltpu.VMEM)
    return pl.pallas_call(
        left_kernel,
        in_specs=[whole] * len(own),
        out_specs=whole,
        out_shape=jax.ShapeDtypeStruct((rows // 2, 2 * channels, 2 * windows), jnp.bfloat16),
        compiler_params=pltpu.CompilerParams(vmem_limit_bytes=VMEM_BYTES),
        name="left_side",
    )(*own)


def correlate_kernel(scale, layout, far_ref, left_ref, *refs):
    out_hbm, right_ref, result_ref, sems = refs[-4:]
    bins, _, _, channels, _ = result_ref.shape

    for r in range(ROUNDS):
        far = far_ref[r]

        @pl.when(far % 2 == 1)
        def _():
            for c, (across, _) in enumerate(layout):
                row = 0
                for n, first, count in across:
                    right_ref[r, c, row : row + count] = refs[n][r, first : first + count]
                    row += count

        for at in layout[0][1]:

            @pl.when(far == at)
            def _():
                for c, (_, by_key) in enumerate(layout):
                    row = 0
                    for n in by_key[at]:
                        count = refs[n].shape[0]
                        right_ref[r, c, row : row + count] = refs[n][...]
                        row += count

    def send(bin_no, r):
        return pltpu.make_async_copy(result_ref.at[bin_no, r], out_hbm.at[r, bin_no], sems.at[bin_no, r])

    @pl.loop(0, bins, unroll=4)
    def _(bin_no):
        for r in range(ROUNDS):
            right = jnp.concatenate(
                [right_ref[r, c, 2 * bin_no + part] for c in range(len(layout)) for part in range(2)], axis=0
            )
            product = jnp.dot(left_ref[bin_no], right, preferred_element_type=jnp.float32)
            result_ref[bin_no, r] = (product * scale).reshape(2, channels, channels)
            send(bin_no, r).start()

    @pl.loop(0, bins)
    def _(bin_no):
        for r in range(ROUNDS):
            send(bin_no, r).wait()


def correlate(far, left, found, across, other):
    bins, both, depth = left.shape
    channels = both // 2
    arrays, layout = list(across), []

    def numbered(parts):
        arrays.extend(parts)
        return list(range(len(arrays) - len(parts), len(arrays)))

    for chunk, parts in zip(found, other):
        layout.append((parts, {at: numbered(chunk[at]) for at in sorted(chunk) if at}))
    rows, windows_dev, _ = found[0][0][0].shape
    whole = pl.BlockSpec(memory_space=pltpu.VMEM)
    shape = (ROUNDS, bins, 2, channels, channels)
    flops = 4 * ROUNDS * bins * depth * channels * channels
    scale = 1.0 / math.sqrt(depth // 2)
    return pl.pallas_call(
        functools.partial(correlate_kernel, scale, layout),
        in_specs=[pl.BlockSpec(memory_space=pltpu.SMEM)] + [whole] * (1 + len(arrays)),
        out_specs=pl.BlockSpec(memory_space=pl.ANY),
        out_shape=jax.ShapeDtypeStruct(shape, jnp.float32),
        scratch_shapes=[
            pltpu.VMEM((ROUNDS, len(layout), rows, windows_dev, channels), jnp.bfloat16),
            pltpu.VMEM((bins, ROUNDS, 2, channels, channels), jnp.float32),
            pltpu.SemaphoreType.DMA((bins, ROUNDS)),
        ],
        compiler_params=pltpu.CompilerParams(vmem_limit_bytes=VMEM_BYTES),
        cost_estimate=pl.CostEstimate(flops=flops, bytes_accessed=4 * math.prod(shape), transcendentals=0),
        name="cross_spectra",
    )(far, left, *arrays)


def partner_positions(partner, block_ids, count):
    slots = jnp.arange(count, dtype=jnp.int32)
    holder = jnp.sum(jnp.where(block_ids[None, :] == slots[:, None], slots[None, :], 0), axis=1)
    at_block = block_ids[:, None] == slots[None, :]
    wanted = jnp.sum(jnp.where(at_block[None], partner[:, None, :], 0), axis=2)
    return jnp.sum(jnp.where(wanted[:, :, None] == slots, holder, 0), axis=2)


def swap(value, axis, distance):
    count = lax.axis_size(axis)
    return lax.ppermute(value, axis, [(i, i ^ distance) for i in range(count)])


def after(value, *others):
    return lax.optimization_barrier((value, *others))[0] if others else value


def gather_even(piece, relay):
    pair_count = lax.axis_size("pair")
    half = piece.shape[0] // 2
    found = {0: [piece]}
    for distance in range(2, pair_count, 2):
        if distance != 6 or not relay:
            found[distance] = [swap(piece, "pair", distance)]
    if relay and 6 < pair_count:
        found[6] = [swap(found[4][0][:half], "pair", 2), swap(found[2][0][half:], "pair", 4)]
    return found


def local(traces, partner, block_ids):
    pair_count = lax.axis_size("pair")
    win_count = lax.axis_size("win")
    rows = 2 * BINS // win_count
    windows = traces.shape[1] * win_count
    me = lax.axis_index("pair")
    slots = jnp.arange(pair_count, dtype=jnp.int32)
    paired = partner_positions(partner, block_ids, pair_count)
    mine = jnp.sum(jnp.where(slots == me, paired, 0), axis=1) ^ me
    beside = jnp.sum(jnp.where(slots == (me ^ 1), paired, 0), axis=1) ^ me

    sent = local_spectra(traces, win_count, [(s, 0, rows) for s in range(win_count)])
    own, found = [], []
    for s, piece in enumerate(sent):
        if s:
            piece = swap(after(piece, own[2], own[1]) if s == 3 else piece, "win", s)
        own.append(piece)
    for s, piece in enumerate(own):
        if s >= 1:
            near = [part for at in (2, 4) for part in found[s - 1].get(at, [])]
            piece = after(piece, *(near if s < 3 else near[:1]), *(found[s - 2].get(6, []) if s == 2 else []))
        found.append(gather_even(piece, relay=s > 0))
    left = left_side(own, windows)
    half = rows // 2
    early = [swap(pick([cut(chunk, 0, rows)], beside), "pair", 1) for chunk in found[:-2]]
    late = [
        swap(pick([cut(chunk, at, at + half) for chunk in found[-2:]], beside), "pair", 1)
        for at in (0, half)
    ]
    other = [[(n, 0, rows)] for n in range(len(early))]
    for n in range(2):
        other.append([(len(early) + part, n * half, half) for part in range(2)])
    return correlate(mine, left, found, early + late, other)


def solution(mesh):
    placed = (P("pair", "win", None), P(), P())
    return jax.shard_map(
        local,
        mesh=mesh,
        in_specs=placed,
        out_specs=P(None, "win", None, "pair", None),
        check_vma=False,
    )
```

```python
import functools
import math

import jax
import jax.numpy as jnp
from jax import lax
from jax.experimental import pallas as pl
from jax.experimental.pallas import tpu as pltpu
from jax.sharding import PartitionSpec as P

BINS = 32
FIRST_BIN = 16
BIN_STEP = 8
ROUNDS = 2
LANES = 128
WIN_ROWS = 16
PITCH = 20
VMEM_BYTES = 44 * 1024 * 1024


def fill_table(table_ref):
    samples, columns = table_ref.shape[1], 2 * BINS
    period = samples // math.gcd(FIRST_BIN, BIN_STEP, samples)
    step = 2.0 * math.pi / samples
    sample = lax.broadcasted_iota(jnp.int32, (period, LANES), 0)
    column = lax.broadcasted_iota(jnp.int32, (period, LANES), 1) & (columns - 1)
    freq = FIRST_BIN + BIN_STEP * (column >> 1)
    angle = step * ((sample * freq) & (samples - 1)).astype(jnp.float32)
    waves = jnp.where((column & 1) == 0, jnp.cos(angle), -jnp.sin(angle))
    around = step * sample.astype(jnp.float32)
    cosine, sine = jnp.cos(around), jnp.sin(around)
    low = lax.broadcasted_iota(jnp.int32, (period, LANES), 1) < columns
    for n in range(samples // period):
        turn = 2.0 * math.pi * n * period / samples
        taper = 0.5 - 0.5 * (math.cos(turn) * cosine - math.sin(turn) * sine)
        tapered = taper * waves
        rows = slice(n * period, (n + 1) * period)
        table_ref[0, rows] = jnp.where(low, tapered, 0.0).astype(jnp.bfloat16)
        table_ref[1, rows] = jnp.where(low, 0.0, tapered).astype(jnp.bfloat16)


def spectra_kernel(chan_rows, win_count, pieces, win_ref, traces_ref, *rest):
    outs = rest[: len(pieces)]
    raw_ref, turned_ref, traces_buf, table_ref, sems = rest[len(pieces) :]
    columns = 2 * BINS
    per = columns // win_count
    samples = traces_ref.shape[2]
    steps = LANES // chan_rows
    halves = traces_ref.shape[1] // WIN_ROWS
    rows = chan_rows * WIN_ROWS

    def copy(h, i, g):
        first = g * LANES + i * chan_rows
        return pltpu.make_async_copy(
            traces_ref.at[pl.ds(first, chan_rows), pl.ds(h * WIN_ROWS, WIN_ROWS), :],
            traces_buf.at[h, pl.ds(first, chan_rows)],
            sems.at[h, i, g],
        )

    for h in range(halves):

        @pl.loop(0, steps)
        def _(i):
            copy(h, i, 0).start()
            copy(h, i, 1).start()

    fill_table(table_ref)
    for h in range(halves):

        @pl.loop(0, steps)
        def _(i):
            copy(h, i, 0).wait()
            copy(h, i, 1).wait()
            low = traces_buf[h, pl.ds(i * chan_rows, chan_rows)].reshape(rows, samples)
            high = traces_buf[h, pl.ds(LANES + i * chan_rows, chan_rows)].reshape(rows, samples)
            raw = jnp.dot(low, table_ref[0], preferred_element_type=jnp.float32)
            raw += jnp.dot(high, table_ref[1], preferred_element_type=jnp.float32)
            base = pl.multiple_of(i * (chan_rows * PITCH), 8)
            for c in range(chan_rows):
                raw_ref[pl.ds(base + c * PITCH, WIN_ROWS), :] = raw[c * WIN_ROWS : (c + 1) * WIN_ROWS]

        for w in range(WIN_ROWS):
            turned = raw_ref[pl.ds(w, LANES, stride=PITCH), :].T
            for g in range(2):
                part = turned[g * columns : (g + 1) * columns]
                power = jnp.mean(part * part, axis=0, keepdims=True)
                first = g * columns * PITCH + w
                turned_ref[pl.ds(first, columns, stride=PITCH), :] = part * lax.rsqrt(power + 1e-05)
        for out_ref, (s, low, high) in zip(outs, pieces):
            base = pl.multiple_of((win_ref[0] ^ s) * (per * PITCH), 8)
            for g in range(2):
                for k in range(low, high):
                    taken = turned_ref[pl.ds(base + (g * columns + k) * PITCH, WIN_ROWS), :]
                    out_ref[k - low, h * WIN_ROWS : (h + 1) * WIN_ROWS, g * LANES : (g + 1) * LANES] = (
                        taken.astype(jnp.bfloat16)
                    )


def local_spectra(traces, win_count, pieces):
    channels, windows, samples = traces.shape
    columns = 2 * BINS
    chan_rows = 64
    steps, halves = LANES // chan_rows, windows // WIN_ROWS
    flops = 2 * channels * windows * samples * columns
    return pl.pallas_call(
        functools.partial(spectra_kernel, chan_rows, win_count, pieces),
        in_specs=[
            pl.BlockSpec(memory_space=pltpu.SMEM),
            pl.BlockSpec(memory_space=pl.ANY),
        ],
        out_specs=[pl.BlockSpec(memory_space=pltpu.VMEM)] * len(pieces),
        out_shape=[
            jax.ShapeDtypeStruct((high - low, windows, channels), jnp.bfloat16) for _, low, high in pieces
        ],
        scratch_shapes=[
            pltpu.VMEM((LANES * PITCH, 2 * columns), jnp.float32),
            pltpu.VMEM((2 * columns * PITCH, LANES), jnp.float32),
            pltpu.VMEM((halves, channels, WIN_ROWS, samples), jnp.bfloat16),
            pltpu.VMEM((2, samples, 2 * columns), jnp.bfloat16),
            pltpu.SemaphoreType.DMA((halves, steps, 2)),
        ],
        compiler_params=pltpu.CompilerParams(vmem_limit_bytes=VMEM_BYTES),
        cost_estimate=pl.CostEstimate(flops=flops, bytes_accessed=traces.size * 2, transcendentals=0),
        name="spectra",
    )(lax.axis_index("win").reshape(1), traces)


def cut(found, low, high):
    cuts = {}
    for at, parts in found.items():
        cuts[at], start = [], 0
        for part in parts:
            first, last = max(low, start), min(high, start + part.shape[0])
            if first < last:
                cuts[at].append((part, first - start, last - first))
            start += part.shape[0]
    return cuts


def pick_kernel(places, far_ref, *refs):
    out_ref = refs[-1]
    for r in range(ROUNDS):
        for at in places:

            @pl.when(far_ref[r] == at)
            def _():
                row = 0
                for n, first, count in places[at]:
                    out_ref[r, row : row + count] = refs[n][first : first + count]
                    row += count


def pick(cuts, far):
    arrays, places = [], {at: [] for at in sorted(cuts[0])}
    for chunk in cuts:
        for at in places:
            for part, first, count in chunk[at]:
                places[at].append((len(arrays), first, count))
                arrays.append(part)
    rows = sum(count for _, _, count in places[0])
    whole = pl.BlockSpec(memory_space=pltpu.VMEM)
    return pl.pallas_call(
        functools.partial(pick_kernel, places),
        in_specs=[pl.BlockSpec(memory_space=pltpu.SMEM)] + [whole] * len(arrays),
        out_specs=whole,
        out_shape=jax.ShapeDtypeStruct((ROUNDS, rows, *arrays[0].shape[1:]), jnp.bfloat16),
        compiler_params=pltpu.CompilerParams(vmem_limit_bytes=VMEM_BYTES),
        name="pick",
    )(far, *arrays)


def left_kernel(*refs):
    own, out_ref = refs[:-1], refs[-1]
    channels = out_ref.shape[1] // 2

    @pl.loop(0, out_ref.shape[0])
    def _(bin_no):
        straight, turned = [], []
        for source in own:
            real, imag = source[2 * bin_no], source[2 * bin_no + 1]
            straight += [real, imag]
            turned += [imag, -real]
        out_ref[bin_no, :channels] = jnp.concatenate(straight, axis=0).T
        out_ref[bin_no, channels:] = jnp.concatenate(turned, axis=0).T


def left_side(own, windows):
    rows, _, channels = own[0].shape
    whole = pl.BlockSpec(memory_space=pltpu.VMEM)
    return pl.pallas_call(
        left_kernel,
        in_specs=[whole] * len(own),
        out_specs=whole,
        out_shape=jax.ShapeDtypeStruct((rows // 2, 2 * channels, 2 * windows), jnp.bfloat16),
        compiler_params=pltpu.CompilerParams(vmem_limit_bytes=VMEM_BYTES),
        name="left_side",
    )(*own)


def correlate_kernel(scale, layout, far_ref, left_ref, *refs):
    out_hbm, right_ref, result_ref, sems = refs[-4:]
    bins, _, _, channels, _ = result_ref.shape

    for r in range(ROUNDS):
        far = far_ref[r]

        @pl.when(far % 2 == 1)
        def _():
            for c, (across, _) in enumerate(layout):
                row = 0
                for n, first, count in across:
                    right_ref[r, c, row : row + count] = refs[n][r, first : first + count]
                    row += count

        for at in layout[0][1]:

            @pl.when(far == at)
            def _():
                for c, (_, by_key) in enumerate(layout):
                    row = 0
                    for n in by_key[at]:
                        count = refs[n].shape[0]
                        right_ref[r, c, row : row + count] = refs[n][...]
                        row += count

    def send(bin_no, r):
        return pltpu.make_async_copy(result_ref.at[bin_no, r], out_hbm.at[r, bin_no], sems.at[bin_no, r])

    @pl.loop(0, bins, unroll=2)
    def _(bin_no):
        for r in range(ROUNDS):
            right = jnp.concatenate(
                [right_ref[r, c, 2 * bin_no + part] for c in range(len(layout)) for part in range(2)], axis=0
            )
            product = jnp.dot(left_ref[bin_no], right, preferred_element_type=jnp.float32)
            result_ref[bin_no, r] = (product * scale).reshape(2, channels, channels)
            send(bin_no, r).start()

    @pl.loop(0, bins)
    def _(bin_no):
        for r in range(ROUNDS):
            send(bin_no, r).wait()


def correlate(far, left, found, across, other):
    bins, both, depth = left.shape
    channels = both // 2
    arrays, layout = list(across), []

    def numbered(parts):
        arrays.extend(parts)
        return list(range(len(arrays) - len(parts), len(arrays)))

    for chunk, parts in zip(found, other):
        layout.append((parts, {at: numbered(chunk[at]) for at in sorted(chunk) if at}))
    rows, windows_dev, _ = found[0][0][0].shape
    whole = pl.BlockSpec(memory_space=pltpu.VMEM)
    shape = (ROUNDS, bins, 2, channels, channels)
    flops = 4 * ROUNDS * bins * depth * channels * channels
    scale = 1.0 / math.sqrt(depth // 2)
    return pl.pallas_call(
        functools.partial(correlate_kernel, scale, layout),
        in_specs=[pl.BlockSpec(memory_space=pltpu.SMEM)] + [whole] * (1 + len(arrays)),
        out_specs=pl.BlockSpec(memory_space=pl.ANY),
        out_shape=jax.ShapeDtypeStruct(shape, jnp.float32),
        scratch_shapes=[
            pltpu.VMEM((ROUNDS, len(layout), rows, windows_dev, channels), jnp.bfloat16),
            pltpu.VMEM((bins, ROUNDS, 2, channels, channels), jnp.float32),
            pltpu.SemaphoreType.DMA((bins, ROUNDS)),
        ],
        compiler_params=pltpu.CompilerParams(vmem_limit_bytes=VMEM_BYTES),
        cost_estimate=pl.CostEstimate(flops=flops, bytes_accessed=4 * math.prod(shape), transcendentals=0),
        name="cross_spectra",
    )(far, left, *arrays)


def partner_positions(partner, block_ids, count):
    slots = jnp.arange(count, dtype=jnp.int32)
    holder = jnp.sum(jnp.where(block_ids[None, :] == slots[:, None], slots[None, :], 0), axis=1)
    at_block = block_ids[:, None] == slots[None, :]
    wanted = jnp.sum(jnp.where(at_block[None], partner[:, None, :], 0), axis=2)
    return jnp.sum(jnp.where(wanted[:, :, None] == slots, holder, 0), axis=2)


def swap(value, axis, distance):
    count = lax.axis_size(axis)
    return lax.ppermute(value, axis, [(i, i ^ distance) for i in range(count)])


def after(value, *others):
    return lax.optimization_barrier((value, *others))[0] if others else value


def gather_even(piece, relay):
    pair_count = lax.axis_size("pair")
    half = piece.shape[0] // 2
    found = {0: [piece]}
    for distance in range(2, pair_count, 2):
        if distance != 6 or not relay:
            found[distance] = [swap(piece, "pair", distance)]
    if relay and 6 < pair_count:
        found[6] = [swap(found[2][0][:half], "pair", 4), swap(found[4][0][half:], "pair", 2)]
    return found


def local(traces, partner, block_ids):
    pair_count = lax.axis_size("pair")
    win_count = lax.axis_size("win")
    rows = 2 * BINS // win_count
    windows = traces.shape[1] * win_count
    me = lax.axis_index("pair")
    slots = jnp.arange(pair_count, dtype=jnp.int32)
    paired = partner_positions(partner, block_ids, pair_count)
    mine = jnp.sum(jnp.where(slots == me, paired, 0), axis=1) ^ me
    beside = jnp.sum(jnp.where(slots == (me ^ 1), paired, 0), axis=1) ^ me

    sent = local_spectra(traces, win_count, [(s, 0, rows) for s in range(win_count)])
    own, found = [], []
    for s, piece in enumerate(sent):
        if s:
            piece = swap(after(piece, own[2], own[1]) if s == 3 else piece, "win", s)
        own.append(piece)
    for s, piece in enumerate(own):
        if s >= 1:
            near = [part for at in (2, 4) for part in found[s - 1].get(at, [])]
            piece = after(piece, *(near if s < 3 else near[:1]), *(found[s - 2].get(6, []) if s == 2 else []))
        found.append(gather_even(piece, relay=s > 0))
    left = left_side(own, windows)
    half = rows // 2
    early = [swap(pick([cut(chunk, 0, rows)], beside), "pair", 1) for chunk in found[:-2]]
    late = [
        swap(pick([cut(chunk, at, at + half) for chunk in found[-2:]], beside), "pair", 1)
        for at in (0, half)
    ]
    other = [[(n, 0, rows)] for n in range(len(early))]
    for n in range(2):
        other.append([(len(early) + part, n * half, half) for part in range(2)])
    return correlate(mine, left, found, early + late, other)


def solution(mesh):
    placed = (P("pair", "win", None), P(), P())
    return jax.shard_map(
        local,
        mesh=mesh,
        in_specs=placed,
        out_specs=P(None, "win", None, "pair", None),
        check_vma=False,
    )
```
